512 devices in a mesh: section: 32 (over z, core), tensor: 2 (over y_lo), dp: 8 (over x, y_hi).
Axes of the slice: x: 4, y: 4 (y_hi: 2, y_lo: 2; y = y_hi * 2 + y_lo), z: 16, core: 2. Of those that a mesh axis runs over, the one named last changes fastest.
Arguments:
- residual: bfloat16 [256, 2304], P(('tensor', 'dp')), may hold values from -6 to 6
- final_gain: float32 [2304], replicated, may hold values from 0.5 to 1.5
- table: bfloat16 [256000, 2304], P(('section', 'tensor', 'dp')), may hold values from -1.1953125 to 1.1953125
- targets: int32 [256], replicated, may hold values from 0 to 255999
- input_ids: int32 [256], replicated, may hold values from 0 to 255999
- loss_mask: int32 [256], replicated, may hold values 0 or 1
- embed_cotangent: bfloat16 [256, 2304], P(('tensor', 'dp')), may hold values from -0.119628906 to 0.119628906
Outputs:
- grad_residual: bfloat16 [256, 2304], P(('tensor', 'dp'))
- grad_gain: float32 [2304], replicated
- grad_table: bfloat16 [256000, 2304], P(('section', 'tensor', 'dp'))
The draws below stay inside these ranges and needn't reach their ends.
All inputs are finite; a program needn't handle non-finite values.
Results may differ from the reference program's by a relative error of at most 0.0044.
Values may be sent and summed in bfloat16 or wider, within the bound.
No kernel may reach another device: no remote copies, remote signals or barrier semaphores. Data moves between devices by JAX's collectives and lax.ppermute only.
A program may use at most 64 MiB of HBM per device.

```python
import math
import jax
import jax.numpy as jnp
import numpy as np
from jax import lax

D = 2304
TOKENS = 256
VOCAB = 256000


def touch_ends(drawn, key, smallest, largest):
    longest = drawn.shape.index(max(drawn.shape))
    spots = []
    for shift in (0, 1):
        where = [jax.random.randint(jax.random.fold_in(key, axis), (), 0, length) for axis, length in enumerate(drawn.shape)]
        where[longest] = (where[longest] + shift) % drawn.shape[longest]
        spots.append(tuple(where))
    return drawn.at[spots[0]].set(smallest).at[spots[1]].set(largest)


def block_scale(key, dims, cuts, low, largest):
    def one(dim, shards_of):
        draws = jax.random.uniform(jax.random.fold_in(jax.random.fold_in(key, 6), dim), (shards_of,), jnp.float32, low / len(cuts), largest / len(cuts))
        return jnp.repeat(jnp.exp(draws), dims[dim] // shards_of).reshape((-1,) + (1,) * (len(dims) - dim - 1))

    factor_of = one(*cuts[0])
    for cut in cuts[1:]:
        factor_of = factor_of * one(*cut)
    return factor_of


def skewed_wide(key, extent, amount, lean):
    portions = [min(1 << octave, amount + 1 - (1 << octave)) * (1 << 20) // math.isqrt((1 << octave) ** lean) + 1 for octave in range((amount + 1).bit_length()) if 1 << octave <= amount]
    scale = 1 + sum(portions) // (1 << 30)
    listing = np.cumsum(np.array([max(1, weight // scale) for weight in portions]))
    pick = jax.random.randint(jax.random.fold_in(key, 1), extent, 0, int(listing[len(portions) - 1]))
    start = jnp.left_shift(1, jnp.searchsorted(jnp.asarray(listing, jnp.int32), pick, side="right").astype(jnp.int32))
    grade = start - 1 + jax.random.randint(jax.random.fold_in(key, 4), extent, 0, 1 << 30) % jnp.minimum(start, amount + 1 - start)
    return jax.random.permutation(jax.random.fold_in(key, 2), amount)[grade].astype(jnp.int32)


def normal_values(rng, extent, deviation, bound, split=(), held_as=jnp.bfloat16):
    level = block_scale(rng, extent, split, -0.22, 0.18) if split else 1.0
    drawn = jax.random.normal(rng, extent, jnp.float32) * deviation * level
    return jnp.minimum(jnp.maximum(drawn, -bound), bound).astype(held_as)


def setup_inputs(seed: int = 0) -> dict:
    seeds = jax.random.split(jax.random.key(seed), 8)
    return {
        "residual": normal_values(seeds[0], (TOKENS, D), 1.0, 6.0, ((0, 16),)),
        "final_gain": jnp.clip(1.0 + 0.1 * jax.random.normal(seeds[1], (D,), jnp.float32), 0.5, 1.5),
        "table": normal_values(seeds[2], (VOCAB, D), 0.2, 1.1953125, ((0, 512),)),
        "targets": touch_ends(skewed_wide(seeds[3], (TOKENS,), VOCAB, 2), jax.random.fold_in(seeds[3], 3), 0, VOCAB - 1).astype(jnp.int32),
        "input_ids": touch_ends(skewed_wide(seeds[4], (TOKENS,), VOCAB, 2), jax.random.fold_in(seeds[4], 3), 0, VOCAB - 1).astype(jnp.int32),
        "loss_mask": touch_ends((jax.random.randint(seeds[5], (TOKENS,), 0, 3) < 2).astype(jnp.int32), jax.random.fold_in(seeds[5], 1), 0, 1),
        "embed_cotangent": normal_values(seeds[6], (TOKENS, D), 0.02, 0.119628906, ((0, 16),)),
    }


def reference(residual, final_gain, table, targets, input_ids, loss_mask, embed_cotangent):
    stream = residual.astype(jnp.float32)
    root_mean = jnp.sqrt(lax.optimization_barrier(jnp.mean(stream * stream, axis=-1, keepdims=True)) + 1e-06)
    normed = stream / root_mean
    hidden = (normed * final_gain).astype(jnp.bfloat16)
    block_size = VOCAB // 32
    table_blocks = table.reshape(32, block_size, D)
    offsets = jnp.arange(32, dtype=jnp.int32) * block_size
    contract = (((1,), (1,)), ((), ()))
    first_dims = (((0,), (0,)), ((), ()))

    def block_total(block_rows):
        scores = lax.dot_general(hidden, block_rows, contract, preferred_element_type=jnp.float32)
        capped = 30.0 * jnp.tanh(scores / 30.0)
        return lax.optimization_barrier(jnp.sum(jnp.exp(capped), axis=1))
    totals = lax.optimization_barrier(jnp.sum(lax.map(block_total, table_blocks), axis=0))
    weight = loss_mask.astype(jnp.float32)[:, None]
    scale = math.sqrt(D)

    def vocab_step(running, pieces):
        block_rows, offset = pieces
        scores = lax.dot_general(hidden, block_rows, contract, preferred_element_type=jnp.float32)
        capped = 30.0 * jnp.tanh(scores / 30.0)
        columns = offset + jnp.arange(block_size, dtype=jnp.int32)
        target_hit = (targets[:, None] == columns[None, :]).astype(jnp.float32)
        dlogits = (weight * (jnp.exp(capped) / totals[:, None] - target_hit) * (1.0 - (capped / 30.0) ** 2)).astype(jnp.bfloat16)
        running = running + jnp.dot(dlogits, block_rows, preferred_element_type=jnp.float32)
        onehot_in = (input_ids[:, None] == columns[None, :]).astype(jnp.bfloat16)
        head_part = lax.dot_general(dlogits, hidden, first_dims, preferred_element_type=jnp.float32)
        input_part = lax.dot_general(onehot_in, embed_cotangent, first_dims, preferred_element_type=jnp.float32)
        return (running, (head_part + scale * input_part).astype(jnp.bfloat16))
    grad_hidden, grad_blocks = lax.scan(vocab_step, jnp.zeros((TOKENS, D), jnp.float32), (table_blocks, offsets))
    scaled = grad_hidden * final_gain
    grad_residual = ((scaled - normed * lax.optimization_barrier(jnp.mean(scaled * normed, axis=-1, keepdims=True))) / root_mean).astype(jnp.bfloat16)
    grad_gain = lax.optimization_barrier(jnp.sum(grad_hidden * normed, axis=0))
    return (grad_residual, grad_gain, grad_blocks.reshape(VOCAB, D))
```

```python
import math

import jax
import jax.numpy as jnp
from jax import lax
from jax.sharding import PartitionSpec as P

PLANE = ("tensor", "dp")
EVERY = ("section", "tensor", "dp")


def exchange(pieces, axes):
    return lax.all_to_all(pieces, axes, 0, 0, tiled=True)


def to_all(x, axes):
    return exchange(jnp.broadcast_to(x[None], (lax.axis_size(axes),) + x.shape), axes)


def on_device(residual, final_gain, table, targets, input_ids, loss_mask, embed_cotangent):
    own, width = residual.shape
    vocab_rows = table.shape[0]
    n_plane, n_section = lax.axis_size(PLANE), lax.axis_size("section")
    tokens = own * n_plane
    all_cotangent = lax.all_gather(embed_cotangent, PLANE, axis=0, tiled=True)

    stream = to_all(residual, PLANE).reshape(tokens, width).astype(jnp.float32)
    root_mean = jnp.sqrt(jnp.mean(stream * stream, axis=-1, keepdims=True) + 1e-06)
    normed = stream / root_mean
    hidden = (normed * final_gain).astype(jnp.bfloat16)

    contract = (((1,), (1,)), ((), ()))
    first_dims = (((0,), (0,)), ((), ()))
    scores = lax.dot_general(hidden, table, contract, preferred_element_type=jnp.float32)
    capped = 30.0 * jnp.tanh(scores / 30.0)
    expterm = jnp.exp(capped)
    sums = jnp.sum(expterm, axis=1)
    sums = jnp.sum(to_all(sums, "section"), axis=0)
    totals = jnp.sum(to_all(sums, PLANE), axis=0)

    columns = lax.axis_index(EVERY) * vocab_rows + jnp.arange(vocab_rows, dtype=jnp.int32)
    target_hit = (targets[:, None] == columns[None, :]).astype(jnp.float32)
    weight = loss_mask.astype(jnp.float32)[:, None]
    dlogits = (
        weight * (expterm / totals[:, None] - target_hit) * (1.0 - (capped / 30.0) ** 2)
    ).astype(jnp.bfloat16)

    partial = jnp.dot(dlogits, table, preferred_element_type=jnp.float32)
    gain_part = jnp.sum(partial * normed, axis=0)
    high = gain_part.astype(jnp.bfloat16)
    low = (gain_part - high.astype(jnp.float32)).astype(jnp.bfloat16)
    rider = jnp.concatenate([high, low]).reshape(own, -1)
    rider_width = rider.shape[1]
    lanes = -(width + rider_width) % 128
    packed = jnp.concatenate(
        [
            partial.astype(jnp.bfloat16).reshape(n_plane, own, width),
            jnp.broadcast_to(rider[None], (n_plane, own, rider_width)),
            jnp.zeros((n_plane, own, lanes), jnp.bfloat16),
        ],
        axis=2,
    )
    arrived = jnp.sum(exchange(packed, PLANE).astype(jnp.float32), axis=0)
    grad_own = arrived[:, :width]
    gain_plane = arrived[:, width : width + rider_width].reshape(2, width).sum(axis=0)

    split = jnp.concatenate(
        [grad_own.reshape(n_section, -1), gain_plane.reshape(n_section, -1)], axis=1
    )
    summed = to_all(jnp.sum(exchange(split, "section"), axis=0), "section")
    cut = own * width // n_section
    grad_hidden = summed[:, :cut].reshape(own, width)
    grad_gain = summed[:, cut:].reshape(width)

    onehot_in = (input_ids[:, None] == columns[None, :]).astype(jnp.bfloat16)
    head_part = lax.dot_general(dlogits, hidden, first_dims, preferred_element_type=jnp.float32)
    input_part = lax.dot_general(
        onehot_in, all_cotangent, first_dims, preferred_element_type=jnp.float32
    )
    grad_table = (head_part + math.sqrt(width) * input_part).astype(jnp.bfloat16)

    stream = residual.astype(jnp.float32)
    root_mean = jnp.sqrt(jnp.mean(stream * stream, axis=-1, keepdims=True) + 1e-06)
    normed = stream / root_mean
    scaled = grad_hidden * final_gain
    grad_residual = (
        (scaled - normed * jnp.mean(scaled * normed, axis=-1, keepdims=True)) / root_mean
    ).astype(jnp.bfloat16)
    return (grad_residual, grad_gain, grad_table)


def solution(mesh):
    placed = (
        P(PLANE, None),
        P(),
        P(EVERY, None),
        P(),
        P(),
        P(),
        P(PLANE, None),
    )
    return jax.shard_map(
        on_device,
        mesh=mesh,
        in_specs=placed,
        out_specs=(P(PLANE, None), P(), P(EVERY, None)),
        check_vma=False,
    )
```

```python
import math

import jax
import jax.numpy as jnp
from jax import lax
from jax.experimental import pallas as pl
from jax.experimental.pallas import tpu as pltpu
from jax.sharding import PartitionSpec as P

PLANE = ("tensor", "dp")
EVERY = ("section", "tensor", "dp")
LANES = 128
VMEM_LIMIT = 24 * 1024 * 1024
F32 = jnp.float32
BF16 = jnp.bfloat16
VMEM = pl.BlockSpec(memory_space=pltpu.VMEM)
SMEM = pl.BlockSpec(memory_space=pltpu.SMEM)


def exchange(pieces, axes):
    return lax.all_to_all(pieces, axes, 0, 0, tiled=True)


def call(body, outs, flops, moved, *operands, in_specs=None, out_specs=None, scratch=()):
    several = isinstance(outs, tuple)
    return pl.pallas_call(
        body,
        out_shape=outs,
        in_specs=in_specs or [VMEM] * len(operands),
        out_specs=out_specs or ((VMEM,) * len(outs) if several else VMEM),
        scratch_shapes=list(scratch),
        compiler_params=pltpu.CompilerParams(vmem_limit_bytes=VMEM_LIMIT),
        cost_estimate=pl.CostEstimate(flops=flops, bytes_accessed=moved, transcendentals=0),
    )(*operands)


def capped_scores(res_ref, gain_ref, table_ref, hidden_ref, inverse_ref):
    tokens = res_ref.shape[0]
    step = 16

    def norm(i, carry):
        rows = pl.ds(pl.multiple_of(i * step, step), step)
        x = res_ref[rows, :].astype(F32)
        inverse = 1.0 / jnp.sqrt(jnp.mean(x * x, axis=1, keepdims=True) + 1e-06)
        inverse_ref[rows, :] = jnp.broadcast_to(inverse, (step, LANES))
        hidden_ref[rows, :] = (x * inverse * gain_ref[...]).astype(BF16)
        return carry

    lax.fori_loop(0, tokens // step, norm, 0, unroll=4)
    scores = lax.dot_general(
        table_ref[...], hidden_ref[...], (((1,), (1,)), ((), ())), preferred_element_type=F32
    )
    return 30.0 * jnp.tanh(scores * (1.0 / 30.0))


def logit_grads(capped, first_ref, arrived_ref, targets_ref, mask_ref):
    totals = arrived_ref[0]
    for i in range(1, arrived_ref.shape[0]):
        totals = totals + arrived_ref[i]
    rows = lax.broadcasted_iota(jnp.int32, capped.shape, 0)
    hit = (targets_ref[...] - first_ref[0] == rows).astype(F32)
    share = jnp.exp(capped) * (1.0 / totals)
    bend = capped * (1.0 / 30.0)
    return (mask_ref[...].astype(F32) * (share - hit) * (1.0 - bend * bend)).astype(BF16)


def sums_body(res_ref, gain_ref, table_ref, sums_ref, hidden_ref, inverse_ref):
    capped = capped_scores(res_ref, gain_ref, table_ref, hidden_ref, inverse_ref)
    sums = jnp.sum(jnp.exp(capped), axis=0, keepdims=True)
    for i in range(sums_ref.shape[0]):
        sums_ref[i] = sums


def spread_body(in_ref, out_ref):
    total = in_ref[0]
    for i in range(1, in_ref.shape[0]):
        total = total + in_ref[i]
    for i in range(out_ref.shape[0]):
        out_ref[i] = total


def partial_body(
    first_ref, arrived_ref, targets_ref, mask_ref, res_ref, gain_ref, table_ref,
    packed_ref, hidden_ref, inverse_ref, rider_ref,
):
    n_plane, own, packed_width = packed_ref.shape
    width = res_ref.shape[1]
    capped = capped_scores(res_ref, gain_ref, table_ref, hidden_ref, inverse_ref)
    dlogits = logit_grads(capped, first_ref, arrived_ref, targets_ref, mask_ref)
    rider_ref[...] = jnp.zeros_like(rider_ref)
    tile = 2 * LANES
    n_lanes = width // LANES
    inverse = jnp.concatenate([inverse_ref[...]] * 2, axis=1)
    for n in range(width // tile):
        columns = slice(n * tile, (n + 1) * tile)
        part = lax.dot_general(
            dlogits, table_ref[:, columns], (((0,), (0,)), ((), ())), preferred_element_type=F32
        )
        packed_ref[:, :, columns] = part.astype(BF16).reshape(n_plane, own, tile)
        normed = res_ref[:, columns].astype(F32) * inverse
        gain = jnp.sum(part * normed, axis=0, keepdims=True)
        high = gain.astype(BF16).astype(F32)
        low = gain - high
        for k in range(2):
            piece = slice(k * LANES, (k + 1) * LANES)
            rider_ref[2 * n + k : 2 * n + k + 1, :] = high[:, piece]
            rider_ref[n_lanes + 2 * n + k : n_lanes + 2 * n + k + 1, :] = low[:, piece]
    for j in range(rider_ref.shape[0] // own):
        block = rider_ref[j * own : (j + 1) * own, :].astype(BF16)
        for i in range(n_plane):
            packed_ref[i, :, width + j * LANES : width + (j + 1) * LANES] = block


def split_body(in_ref, out_ref, gain_ref):
    n_plane, own, packed_width = in_ref.shape
    n_section = out_ref.shape[0]
    cut = out_ref.shape[2] - LANES
    halves = n_section // own
    width = halves * cut
    n_lanes = width // LANES
    total = in_ref[0].astype(F32)
    for i in range(1, n_plane):
        total = total + in_ref[i].astype(F32)
    for h in range(halves):
        out_ref[h * own : (h + 1) * own, 0, :cut] = total[:, h * cut : (h + 1) * cut]
    for j in range((packed_width - width) // LANES):
        gain_ref[j * own : (j + 1) * own, :] = total[:, width + j * LANES : width + (j + 1) * LANES]
    rows = gain_ref[:n_lanes, :] + gain_ref[n_lanes : 2 * n_lanes, :]
    out_ref[:n_lanes, 0, cut:] = rows
    out_ref[n_lanes:, 0, cut:] = jnp.zeros((n_section - n_lanes, LANES), F32)


def finish_body(in_ref, res_ref, gain_ref, grad_ref, grad_gain_ref):
    n_section = in_ref.shape[0]
    own, width = res_ref.shape
    cut = in_ref.shape[2] - LANES
    halves = n_section // own
    x = res_ref[...].astype(F32)
    inverse = 1.0 / jnp.sqrt(jnp.mean(x * x, axis=1, keepdims=True) + 1e-06)
    normed = x * inverse
    grad_hidden = jnp.concatenate(
        [in_ref[h * own : (h + 1) * own, 0, :cut] for h in range(halves)], axis=1
    )
    scaled = grad_hidden * gain_ref[...]
    along = jnp.mean(scaled * normed, axis=1, keepdims=True)
    grad_ref[...] = ((scaled - normed * along) * inverse).astype(BF16)
    grad_gain_ref[...] = in_ref[: width // LANES, 0, cut:]


def table_body(
    first_ref, arrived_ref, targets_ref, mask_ref, res_ref, gain_ref, table_ref, ids_ref,
    cotangent_ref, out_ref, hidden_ref, inverse_ref,
):
    vocab_rows, width = out_ref.shape
    capped = capped_scores(res_ref, gain_ref, table_ref, hidden_ref, inverse_ref)
    dlogits = logit_grads(capped, first_ref, arrived_ref, targets_ref, mask_ref)
    rows = lax.broadcasted_iota(jnp.int32, capped.shape, 0)
    onehot = (ids_ref[...] - first_ref[0] == rows).astype(F32).astype(BF16)
    scale = math.sqrt(width)
    tile = 2 * LANES
    for n in range(width // tile):
        columns = slice(n * tile, (n + 1) * tile)
        head = jnp.dot(dlogits, hidden_ref[:, columns], preferred_element_type=F32)
        inputs = jnp.dot(onehot, cotangent_ref[:, columns], preferred_element_type=F32)
        out_ref[:, columns] = (head + scale * inputs).astype(BF16)


def on_device(residual, final_gain, table, targets, input_ids, loss_mask, embed_cotangent):
    own, width = residual.shape
    vocab_rows = table.shape[0]
    n_plane, n_section = lax.axis_size(PLANE), lax.axis_size("section")
    tokens = own * n_plane
    cut = own * width // n_section
    n_lanes = width // LANES
    rider = -(-2 * n_lanes // own) * own
    product = 2 * tokens * vocab_rows * width
    shape = jax.ShapeDtypeStruct
    first = (lax.axis_index(EVERY) * vocab_rows).astype(jnp.int32).reshape(1)
    gain_row = final_gain.reshape(1, width)

    packed_width = width + rider // own * LANES
    norm_rooms = [pltpu.VMEM((tokens, width), BF16), pltpu.VMEM((tokens, LANES), F32)]
    rows_bytes = vocab_rows * width * 2

    wide = jnp.pad(embed_cotangent, ((0, 0), (0, 512)))
    everyone = exchange(jnp.broadcast_to(residual[None], (n_plane, own, width)), PLANE)
    everyone = everyone.reshape(tokens, width)
    everyone, wide = lax.optimization_barrier((everyone, wide))
    all_cotangent = lax.all_gather(wide, PLANE, axis=0, tiled=True)

    sums = call(
        sums_body,
        shape((n_section, 1, tokens), F32),
        product,
        rows_bytes,
        everyone, gain_row, table,
        scratch=norm_rooms,
    )
    sums = call(
        spread_body, shape((n_plane, 1, tokens), F32), tokens, 4 * tokens, exchange(sums, "section")
    )
    given = (
        first, exchange(sums, PLANE), targets.reshape(1, tokens), loss_mask.reshape(1, tokens),
        everyone, gain_row, table,
    )
    packed = call(
        partial_body,
        shape((n_plane, own, packed_width), BF16),
        2 * product,
        rows_bytes,
        *given,
        in_specs=[SMEM] + [VMEM] * 6,
        scratch=norm_rooms + [pltpu.VMEM((rider, LANES), F32)],
    )
    arrived = exchange(packed, PLANE)
    split = call(
        split_body,
        shape((n_section, 1, cut + LANES), F32),
        tokens * width,
        tokens * width * 2,
        arrived,
        scratch=[pltpu.VMEM((rider, LANES), F32)],
    )
    reduced = call(
        spread_body,
        shape((n_section, 1, cut + LANES), F32),
        own * width,
        own * width * 8,
        exchange(split, "section"),
    )
    grad_table = call(
        table_body,
        shape((vocab_rows, width), BF16),
        3 * product,
        2 * rows_bytes,
        *given, input_ids.reshape(1, tokens), all_cotangent,
        in_specs=[SMEM] + [VMEM] * 8,
        scratch=norm_rooms,
    )
    summed, grad_table = lax.optimization_barrier((exchange(reduced, "section"), grad_table))
    grad_residual, grad_gain = call(
        finish_body,
        (shape((own, width), BF16), shape((n_lanes, LANES), F32)),
        own * width * 10,
        own * width * 8,
        summed, residual, gain_row,
    )
    return (grad_residual, grad_gain.reshape(width), grad_table)


def solution(mesh):
    placed = (
        P(PLANE, None),
        P(),
        P(EVERY, None),
        P(),
        P(),
        P(),
        P(PLANE, None),
    )
    return jax.shard_map(
        on_device,
        mesh=mesh,
        in_specs=placed,
        out_specs=(P(PLANE, None), P(), P(EVERY, None)),
        check_vma=False,
    )
```

```python
import math

import jax
import jax.numpy as jnp
from jax import lax
from jax.experimental import pallas as pl
from jax.experimental.pallas import tpu as pltpu
from jax.sharding import PartitionSpec as P

PLANE = ("tensor", "dp")
EVERY = ("section", "tensor", "dp")
LANES = 128
SLOTS = 3
VMEM_LIMIT = 24 * 1024 * 1024
F32 = jnp.float32
BF16 = jnp.bfloat16
VMEM = pl.BlockSpec(memory_space=pltpu.VMEM)
SMEM = pl.BlockSpec(memory_space=pltpu.SMEM)


def exchange(pieces, axes):
    return lax.all_to_all(pieces, axes, 0, 0, tiled=True)


def call(body, outs, flops, moved, *operands, in_specs=None, out_specs=None, scratch=()):
    several = isinstance(outs, tuple)
    return pl.pallas_call(
        body,
        out_shape=outs,
        in_specs=in_specs or [VMEM] * len(operands),
        out_specs=out_specs or ((VMEM,) * len(outs) if several else VMEM),
        scratch_shapes=list(scratch),
        compiler_params=pltpu.CompilerParams(vmem_limit_bytes=VMEM_LIMIT),
        cost_estimate=pl.CostEstimate(flops=flops, bytes_accessed=moved, transcendentals=0),
    )(*operands)


def capped_scores(res_ref, gain_ref, table_ref, hidden_ref, inverse_ref):
    tokens = res_ref.shape[0]
    step = 16

    def norm(i, carry):
        rows = pl.ds(pl.multiple_of(i * step, step), step)
        x = res_ref[rows, :].astype(F32)
        inverse = 1.0 / jnp.sqrt(jnp.mean(x * x, axis=1, keepdims=True) + 1e-06)
        inverse_ref[rows, :] = jnp.broadcast_to(inverse, (step, LANES))
        hidden_ref[rows, :] = (x * inverse * gain_ref[...]).astype(BF16)
        return carry

    lax.fori_loop(0, tokens // step, norm, 0, unroll=4)
    scores = lax.dot_general(
        table_ref[...], hidden_ref[...], (((1,), (1,)), ((), ())), preferred_element_type=F32
    )
    return 30.0 * jnp.tanh(scores * (1.0 / 30.0))


def logit_grads(capped, first_ref, arrived_ref, targets_ref, mask_ref):
    totals = arrived_ref[0]
    for i in range(1, arrived_ref.shape[0]):
        totals = totals + arrived_ref[i]
    rows = lax.broadcasted_iota(jnp.int32, capped.shape, 0)
    hit = (targets_ref[...] - first_ref[0] == rows).astype(F32)
    share = jnp.exp(capped) * (1.0 / totals)
    bend = capped * (1.0 / 30.0)
    return (mask_ref[...].astype(F32) * (share - hit) * (1.0 - bend * bend)).astype(BF16)


def sums_body(res_ref, gain_ref, table_ref, sums_ref, hidden_ref, inverse_ref):
    capped = capped_scores(res_ref, gain_ref, table_ref, hidden_ref, inverse_ref)
    sums = jnp.sum(jnp.exp(capped), axis=0, keepdims=True)
    for i in range(sums_ref.shape[0]):
        sums_ref[i] = sums


def spread_body(in_ref, out_ref):
    total = in_ref[0]
    for i in range(1, in_ref.shape[0]):
        total = total + in_ref[i]
    for i in range(out_ref.shape[0]):
        out_ref[i] = total


def partial_body(
    first_ref, arrived_ref, targets_ref, mask_ref, res_ref, gain_ref, table_ref,
    packed_ref, hidden_ref, inverse_ref, rider_ref,
):
    n_plane, own, packed_width = packed_ref.shape
    width = res_ref.shape[1]
    capped = capped_scores(res_ref, gain_ref, table_ref, hidden_ref, inverse_ref)
    dlogits = logit_grads(capped, first_ref, arrived_ref, targets_ref, mask_ref)
    rider_ref[...] = jnp.zeros_like(rider_ref)
    tile = 2 * LANES
    n_lanes = width // LANES
    inverse = jnp.concatenate([inverse_ref[...]] * 2, axis=1)
    for n in range(width // tile):
        columns = slice(n * tile, (n + 1) * tile)
        part = lax.dot_general(
            dlogits, table_ref[:, columns], (((0,), (0,)), ((), ())), preferred_element_type=F32
        )
        packed_ref[:, :, columns] = part.astype(BF16).reshape(n_plane, own, tile)
        normed = res_ref[:, columns].astype(F32) * inverse
        gain = jnp.sum(part * normed, axis=0, keepdims=True)
        high = gain.astype(BF16).astype(F32)
        low = gain - high
        for k in range(2):
            piece = slice(k * LANES, (k + 1) * LANES)
            rider_ref[2 * n + k : 2 * n + k + 1, :] = high[:, piece]
            rider_ref[n_lanes + 2 * n + k : n_lanes + 2 * n + k + 1, :] = low[:, piece]
    for j in range(rider_ref.shape[0] // own):
        block = rider_ref[j * own : (j + 1) * own, :].astype(BF16)
        for i in range(n_plane):
            packed_ref[i, :, width + j * LANES : width + (j + 1) * LANES] = block


def split_body(in_ref, out_ref, gain_ref):
    n_plane, own, packed_width = in_ref.shape
    n_section = out_ref.shape[0]
    cut = out_ref.shape[2] - LANES
    halves = n_section // own
    width = halves * cut
    n_lanes = width // LANES
    total = in_ref[0].astype(F32)
    for i in range(1, n_plane):
        total = total + in_ref[i].astype(F32)
    for h in range(halves):
        out_ref[h * own : (h + 1) * own, 0, :cut] = total[:, h * cut : (h + 1) * cut]
    for j in range((packed_width - width) // LANES):
        gain_ref[j * own : (j + 1) * own, :] = total[:, width + j * LANES : width + (j + 1) * LANES]
    rows = gain_ref[:n_lanes, :] + gain_ref[n_lanes : 2 * n_lanes, :]
    out_ref[:n_lanes, 0, cut:] = rows
    out_ref[n_lanes:, 0, cut:] = jnp.zeros((n_section - n_lanes, LANES), F32)


def finish_body(in_ref, res_ref, gain_ref, grad_ref, grad_gain_ref):
    n_section = in_ref.shape[0]
    own, width = res_ref.shape
    cut = in_ref.shape[2] - LANES
    halves = n_section // own
    x = res_ref[...].astype(F32)
    inverse = 1.0 / jnp.sqrt(jnp.mean(x * x, axis=1, keepdims=True) + 1e-06)
    normed = x * inverse
    grad_hidden = jnp.concatenate(
        [in_ref[h * own : (h + 1) * own, 0, :cut] for h in range(halves)], axis=1
    )
    scaled = grad_hidden * gain_ref[...]
    along = jnp.mean(scaled * normed, axis=1, keepdims=True)
    grad_ref[...] = ((scaled - normed * along) * inverse).astype(BF16)
    grad_gain_ref[...] = in_ref[: width // LANES, 0, cut:]


def table_body(
    first_ref, arrived_ref, targets_ref, mask_ref, res_ref, gain_ref, table_ref, ids_ref,
    cotangent_ref, out_ref, hidden_ref, inverse_ref,
):
    vocab_rows, width = out_ref.shape
    capped = capped_scores(res_ref, gain_ref, table_ref, hidden_ref, inverse_ref)
    dlogits = logit_grads(capped, first_ref, arrived_ref, targets_ref, mask_ref)
    rows = lax.broadcasted_iota(jnp.int32, capped.shape, 0)
    onehot = (ids_ref[...] - first_ref[0] == rows).astype(F32).astype(BF16)
    scale = math.sqrt(width)
    tile = 2 * LANES
    for n in range(width // tile):
        columns = slice(n * tile, (n + 1) * tile)
        head = jnp.dot(dlogits, hidden_ref[:, columns], preferred_element_type=F32)
        inputs = jnp.dot(onehot, cotangent_ref[:, columns], preferred_element_type=F32)
        out_ref[:, columns] = (head + scale * inputs).astype(BF16)


def plan_body(ids_ref, me_ref, rows_ref, codes_ref, most_ref):
    _, own, groups = ids_ref.shape
    section, place, vocab_rows = me_ref[0], me_ref[1], me_ref[2]
    device = section * groups + place
    most = jnp.int32(0)
    for which in range(2):
        ids = ids_ref[which]
        token = lax.broadcasted_iota(jnp.int32, ids.shape, 0)
        group = lax.broadcasted_iota(jnp.int32, ids.shape, 1)
        owner = lax.div(ids, vocab_rows)
        again = jnp.zeros(ids.shape, jnp.int32)
        for j in range(own):
            again = again + jnp.where((ids == ids[j : j + 1]) & (token > j), 1, 0)
        first = jnp.where(again == 0, 1, 0)
        slot = jnp.zeros(ids.shape, jnp.int32)
        for j in range(own):
            under = (owner == owner[j : j + 1]) & (ids[j : j + 1] < ids) & (first[j : j + 1] == 1)
            slot = slot + jnp.where(under, 1, 0)
        most = jnp.maximum(most, jnp.max(slot))
        rows_ref[which] = jnp.full(rows_ref.shape[1:], -1, jnp.int32)
        mine = (owner == device) & (first == 1)
        for k in range(SLOTS):
            local = jnp.where(mine & (slot == k), ids - device * vocab_rows + 1, 0)
            rows_ref[which, :, k * groups : (k + 1) * groups] = (
                jnp.sum(local, axis=0, keepdims=True) - 1
            )
        near = owner - section * groups
        code = jnp.where((near >= 0) & (near < groups), slot * groups + near, -1)
        code = jnp.sum(jnp.where(group == place, code, 0), axis=1, keepdims=True)
        codes_ref[which] = jnp.broadcast_to(code, codes_ref.shape[1:])
    most_ref[0] = most


def three_terms(x):
    high = x.astype(BF16).astype(F32)
    middle = (x - high).astype(BF16).astype(F32)
    return high, middle, x - high - middle


def slot_layout(own, width, tokens):
    n_lanes = width // LANES
    token_tiles = -(-tokens // LANES)
    scalars = 2 * SLOTS * n_lanes
    tiles = -(-(scalars + 6 * token_tiles) // own)
    return n_lanes, token_tiles, scalars, tiles


def compact_body(
    res_ref, gain_ref, table_ref, target_row_ref, mask_ref, slot_rows_ref, codes_ref, cotangent_ref,
    packed_ref, hidden_ref, inverse_ref, tokens_ref, room_ref,
):
    n_plane, own, packed_width = packed_ref.shape
    tokens, width = res_ref.shape
    vocab_rows = table_ref.shape[0]
    n_lanes, token_tiles, scalars, tiles = slot_layout(own, width, tokens)
    capped = capped_scores(res_ref, gain_ref, table_ref, hidden_ref, inverse_ref)
    rows = lax.broadcasted_iota(jnp.int32, capped.shape, 0)
    hit = target_row_ref[...] == rows
    expterm = jnp.exp(capped)
    bend = capped * (1.0 / 30.0)
    weight = mask_ref[...].astype(F32) * (1.0 - bend * bend)
    unscaled = jnp.where(hit, 0.0, weight * expterm).astype(BF16)
    pieces = [
        jnp.sum(expterm, axis=0, keepdims=True),
        jnp.sum(jnp.where(hit, capped, 0.0), axis=0, keepdims=True),
    ]
    stride = tiles * own

    def put(at, value):
        room_ref[pl.ds(at, n_plane, stride=stride), :] = value

    used = scalars + 6 * token_tiles
    for at in range(used, stride):
        put(at, jnp.zeros((n_plane, LANES), F32))
    tokens_ref[...] = jnp.zeros_like(tokens_ref)
    for which in range(2):
        for term, value in enumerate(three_terms(pieces[which])):
            tokens_ref[:, :tokens] = value
            for t in range(token_tiles):
                at = scalars + (which * 3 + term) * token_tiles + t
                row = tokens_ref[:, t * LANES : (t + 1) * LANES]
                put(at, jnp.broadcast_to(row, (n_plane, LANES)))

    n_slots = SLOTS * n_plane
    slot_iota = lax.broadcasted_iota(jnp.int32, (vocab_rows, n_slots), 0)
    pick = (slot_rows_ref[0, :, :n_slots] == slot_iota).astype(F32).astype(BF16)
    own_iota = lax.broadcasted_iota(jnp.int32, (own, n_slots), 1)
    give = (codes_ref[1, :, :n_slots] == own_iota).astype(F32).astype(BF16)
    dims = (((0,), (0,)), ((), ()))
    tile = 2 * LANES
    for n in range(width // tile):
        columns = slice(n * tile, (n + 1) * tile)
        part = lax.dot_general(unscaled, table_ref[:, columns], dims, preferred_element_type=F32)
        packed_ref[:, :, columns] = part.astype(BF16).reshape(n_plane, own, tile)
        moved = (
            lax.dot_general(pick, table_ref[:, columns], dims, preferred_element_type=F32),
            lax.dot_general(give, cotangent_ref[:, columns], dims, preferred_element_type=F32),
        )
        for which in range(2):
            for k in range(SLOTS):
                for half in range(2):
                    at = (which * SLOTS + k) * n_lanes + 2 * n + half
                    put(at, moved[which][k * n_plane : (k + 1) * n_plane, half * LANES : (half + 1) * LANES])
    for p in range(n_plane):
        for t in range(tiles):
            start = p * stride + t * own
            packed_ref[p, :, width + t * LANES : width + (t + 1) * LANES] = (
                room_ref[start : start + own, :].astype(BF16)
            )


def unpack_body(
    in_ref, place_ref, codes_ref, out_ref, rows_out_ref, room_ref, moved_ref, rest_ref
):
    n_plane, own, packed_width = in_ref.shape
    tokens = n_plane * own
    n_section = out_ref.shape[0]
    halves = n_section // own
    width = rows_out_ref.shape[1]
    cut = width // halves
    n_lanes, token_tiles, scalars, tiles = slot_layout(own, width, tokens)
    stride = tiles * own
    total = in_ref[0, :, :width].astype(F32)
    for p in range(1, n_plane):
        total = total + in_ref[p, :, :width].astype(F32)
    for p in range(n_plane):
        for t in range(tiles):
            start = p * stride + t * own
            room_ref[start : start + own, :] = in_ref[
                p, :, width + t * LANES : width + (t + 1) * LANES
            ].astype(F32)

    def take(at):
        return room_ref[pl.ds(at, n_plane, stride=stride), :]

    for which in range(2):
        for k in range(SLOTS):
            for j in range(n_lanes):
                moved_ref[
                    which, k * n_plane : (k + 1) * n_plane, j * LANES : (j + 1) * LANES
                ] = take((which * SLOTS + k) * n_lanes + j)
    rows_out_ref[...] = moved_ref[1].astype(BF16)
    n_slots = SLOTS * n_plane
    own_iota = lax.broadcasted_iota(jnp.int32, (own, n_slots), 1)
    choose = (codes_ref[0, :, :n_slots] == own_iota).astype(F32).astype(BF16)
    target_rows = jnp.dot(choose, moved_ref[0].astype(BF16), preferred_element_type=F32)
    for h in range(halves):
        for i in range(own):
            s = h * own + i
            rest_ref[2 * s : 2 * s + 1, :cut] = total[i : i + 1, h * cut : (h + 1) * cut]
            rest_ref[2 * s + 1 : 2 * s + 2, :cut] = target_rows[i : i + 1, h * cut : (h + 1) * cut]

    def summed(which):
        tiles_of = []
        for t in range(token_tiles):
            terms = [
                jnp.sum(take(scalars + (which * 3 + term) * token_tiles + t), axis=0, keepdims=True)
                for term in range(3)
            ]
            tiles_of.append(terms[0] + terms[1] + terms[2])
        return tiles_of

    lane = lax.broadcasted_iota(jnp.int32, (own, LANES), 1)
    token = lax.broadcasted_iota(jnp.int32, (own, LANES), 0) + place_ref[0] * own
    score = jnp.zeros((own, 1), F32)
    for t, value in enumerate(summed(1)):
        score = score + jnp.sum(
            jnp.where(lane + t * LANES == token, jnp.broadcast_to(value, lane.shape), 0.0),
            axis=1,
            keepdims=True,
        )
    high, middle, low = three_terms(score)
    scores = jnp.where(lane == 0, high, jnp.where(lane == 1, middle, jnp.where(lane == 2, low, 0.0)))
    sums = [three_terms(value) for value in summed(0)]
    extra = [sums[t][term] for term in range(3) for t in range(token_tiles)]
    per_row = (len(extra) + 2) // 2
    for s in range(n_section):
        i = s % own
        for n, value in enumerate(extra + [scores[i : i + 1]]):
            row, column = 2 * s + n // per_row, cut + n % per_row * LANES
            rest_ref[row : row + 1, column : column + LANES] = value
        for n in range(len(extra) + 1, 2 * per_row):
            row, column = 2 * s + n // per_row, cut + n % per_row * LANES
            rest_ref[row : row + 1, column : column + LANES] = jnp.zeros((1, LANES), F32)
    for s in range(n_section):
        out_ref[s] = rest_ref[2 * s : 2 * s + 2, :].astype(BF16)


def combine_body(in_ref, me_ref, mask_ref, out_ref, totals_ref, tokens_ref):
    n_section, _, piece_width = in_ref.shape
    cut = out_ref.shape[2]
    tokens = totals_ref.shape[1]
    own = me_ref[3]
    total = in_ref[0].astype(F32)
    for s in range(1, n_section):
        total = total + in_ref[s].astype(F32)
    token_tiles = -(-tokens // LANES)
    per_row = (piece_width - cut) // LANES

    def tile_of(n):
        row, column = n // per_row, cut + n % per_row * LANES
        return total[row : row + 1, column : column + LANES]

    for t in range(token_tiles):
        tokens_ref[:, t * LANES : (t + 1) * LANES] = (
            tile_of(t) + tile_of(token_tiles + t) + tile_of(2 * token_tiles + t)
        )
    totals = tokens_ref[:, :tokens]
    totals_ref[...] = totals
    token = me_ref[1] * own + lax.rem(me_ref[0], own)
    here = lax.broadcasted_iota(jnp.int32, totals.shape, 1) == token
    whole = jnp.sum(jnp.where(here, totals, 0.0), axis=1, keepdims=True)
    weight = jnp.sum(jnp.where(here, mask_ref[...].astype(F32), 0.0), axis=1, keepdims=True)
    score = jnp.sum(tile_of(3 * token_tiles), axis=1, keepdims=True)
    bend = score * (1.0 / 30.0)
    at_target = weight * (jnp.exp(score) / whole - 1.0) * (1.0 - bend * bend)
    at_target = at_target.astype(BF16).astype(F32)
    grad = total[0:1, :cut] / whole + at_target * total[1:2, :cut]
    for s in range(out_ref.shape[0]):
        out_ref[s] = grad


def close_body(in_ref, res_ref, gain_ref, grad_ref, gain_out_ref):
    n_section = in_ref.shape[0]
    own, width = res_ref.shape
    halves = n_section // own
    x = res_ref[...].astype(F32)
    inverse = 1.0 / jnp.sqrt(jnp.mean(x * x, axis=1, keepdims=True) + 1e-06)
    normed = x * inverse
    grad_hidden = jnp.concatenate(
        [in_ref[h * own : (h + 1) * own, 0, :] for h in range(halves)], axis=1
    )
    gain = jnp.sum(grad_hidden * normed, axis=0, keepdims=True)
    for p in range(gain_out_ref.shape[0]):
        gain_out_ref[p] = gain
    scaled = grad_hidden * gain_ref[...]
    along = jnp.mean(scaled * normed, axis=1, keepdims=True)
    grad_ref[...] = ((scaled - normed * along) * inverse).astype(BF16)


def compact_table_body(
    target_row_ref, totals_ref, mask_ref, res_ref, gain_ref, table_ref, slot_rows_ref, moved_ref,
    out_ref, hidden_ref, inverse_ref,
):
    vocab_rows, width = out_ref.shape
    capped = capped_scores(res_ref, gain_ref, table_ref, hidden_ref, inverse_ref)
    rows = lax.broadcasted_iota(jnp.int32, capped.shape, 0)
    hit = (target_row_ref[...] == rows).astype(F32)
    share = jnp.exp(capped) * (1.0 / totals_ref[...])
    bend = capped * (1.0 / 30.0)
    dlogits = (mask_ref[...].astype(F32) * (share - hit) * (1.0 - bend * bend)).astype(BF16)
    n_slots = moved_ref.shape[0]
    slot_iota = lax.broadcasted_iota(jnp.int32, (vocab_rows, n_slots), 0)
    onehot = (slot_rows_ref[1, :, :n_slots] == slot_iota).astype(F32).astype(BF16)
    scale = math.sqrt(width)
    tile = 2 * LANES
    for n in range(width // tile):
        columns = slice(n * tile, (n + 1) * tile)
        head = jnp.dot(dlogits, hidden_ref[:, columns], preferred_element_type=F32)
        inputs = jnp.dot(onehot, moved_ref[:, columns], preferred_element_type=F32)
        out_ref[:, columns] = (head + scale * inputs).astype(BF16)


def general(
    everyone, plan, residual, final_gain, table, targets, input_ids, loss_mask, embed_cotangent
):
    del plan
    own, width = residual.shape
    vocab_rows = table.shape[0]
    n_plane, n_section = lax.axis_size(PLANE), lax.axis_size("section")
    tokens = own * n_plane
    cut = own * width // n_section
    n_lanes = width // LANES
    rider = -(-2 * n_lanes // own) * own
    product = 2 * tokens * vocab_rows * width
    shape = jax.ShapeDtypeStruct
    first = (lax.axis_index(EVERY) * vocab_rows).astype(jnp.int32).reshape(1)
    gain_row = final_gain.reshape(1, width)

    packed_width = width + rider // own * LANES
    norm_rooms = [pltpu.VMEM((tokens, width), BF16), pltpu.VMEM((tokens, LANES), F32)]
    rows_bytes = vocab_rows * width * 2

    wide = jnp.pad(embed_cotangent, ((0, 0), (0, 512)))
    all_cotangent = lax.all_gather(wide, PLANE, axis=0, tiled=True)

    sums = call(
        sums_body,
        shape((n_section, 1, tokens), F32),
        product,
        rows_bytes,
        everyone, gain_row, table,
        scratch=norm_rooms,
    )
    sums = call(
        spread_body, shape((n_plane, 1, tokens), F32), tokens, 4 * tokens, exchange(sums, "section")
    )
    given = (
        first, exchange(sums, PLANE), targets.reshape(1, tokens), loss_mask.reshape(1, tokens),
        everyone, gain_row, table,
    )
    packed = call(
        partial_body,
        shape((n_plane, own, packed_width), BF16),
        2 * product,
        rows_bytes,
        *given,
        in_specs=[SMEM] + [VMEM] * 6,
        scratch=norm_rooms + [pltpu.VMEM((rider, LANES), F32)],
    )
    arrived = exchange(packed, PLANE)
    split = call(
        split_body,
        shape((n_section, 1, cut + LANES), F32),
        tokens * width,
        tokens * width * 2,
        arrived,
        scratch=[pltpu.VMEM((rider, LANES), F32)],
    )
    reduced = call(
        spread_body,
        shape((n_section, 1, cut + LANES), F32),
        own * width,
        own * width * 8,
        exchange(split, "section"),
    )
    grad_table = call(
        table_body,
        shape((vocab_rows, width), BF16),
        3 * product,
        2 * rows_bytes,
        *given, input_ids.reshape(1, tokens), all_cotangent,
        in_specs=[SMEM] + [VMEM] * 8,
        scratch=norm_rooms,
    )
    summed, grad_table = lax.optimization_barrier((exchange(reduced, "section"), grad_table))
    grad_residual, grad_gain = call(
        finish_body,
        (shape((own, width), BF16), shape((n_lanes, LANES), F32)),
        own * width * 10,
        own * width * 8,
        summed, residual, gain_row,
    )
    return (grad_residual, grad_gain.reshape(width), grad_table)


def compact(
    everyone, plan, residual, final_gain, table, targets, input_ids, loss_mask, embed_cotangent
):
    del input_ids
    slot_rows, codes, me = plan
    own, width = residual.shape
    vocab_rows = table.shape[0]
    n_plane, n_section = lax.axis_size(PLANE), lax.axis_size("section")
    tokens = own * n_plane
    cut = own * width // n_section
    product = 2 * tokens * vocab_rows * width
    rows_bytes = vocab_rows * width * 2
    shape = jax.ShapeDtypeStruct
    _, token_tiles, _, tiles = slot_layout(own, width, tokens)
    packed_width = width + tiles * LANES
    piece_width = cut + (3 * token_tiles + 2) // 2 * LANES
    norm_rooms = [pltpu.VMEM((tokens, width), BF16), pltpu.VMEM((tokens, LANES), F32)]
    gain_row = final_gain.reshape(1, width)
    mask = loss_mask.reshape(1, tokens)
    target_row = targets.reshape(1, tokens) - (me[0] * n_plane + me[1]) * vocab_rows

    packed = call(
        compact_body,
        shape((n_plane, own, packed_width), BF16),
        2 * product,
        rows_bytes,
        everyone, gain_row, table, target_row, mask, slot_rows, codes, embed_cotangent,
        scratch=norm_rooms + [
            pltpu.VMEM((1, token_tiles * LANES), F32),
            pltpu.VMEM((n_plane * tiles * own, LANES), F32),
        ],
    )
    pieces, moved = call(
        unpack_body,
        (
            shape((n_section, 2, piece_width), BF16),
            shape((SLOTS * n_plane, width), BF16),
        ),
        tokens * width,
        tokens * packed_width * 2,
        exchange(packed, PLANE), me[1:2], codes,
        in_specs=[VMEM, SMEM, VMEM],
        scratch=[
            pltpu.VMEM((n_plane * tiles * own, LANES), F32),
            pltpu.VMEM((2, SLOTS * n_plane, width), F32),
            pltpu.VMEM((2 * n_section, piece_width), F32),
        ],
    )
    half_token, totals = call(
        combine_body,
        (shape((n_section, 1, cut), F32), shape((1, tokens), F32)),
        own * width,
        own * width * 8,
        exchange(pieces, "section"), me, mask,
        in_specs=[VMEM, SMEM, VMEM],
        scratch=[pltpu.VMEM((1, token_tiles * LANES), F32)],
    )
    grad_table = call(
        compact_table_body,
        shape((vocab_rows, width), BF16),
        3 * product,
        2 * rows_bytes,
        target_row, totals, mask, everyone, gain_row, table, slot_rows, moved,
        scratch=norm_rooms,
    )
    summed, grad_table = lax.optimization_barrier((exchange(half_token, "section"), grad_table))
    grad_residual, gain_part = call(
        close_body,
        (shape((own, width), BF16), shape((n_plane, 1, width), F32)),
        own * width * 10,
        own * width * 8,
        summed, residual, gain_row,
    )
    grad_gain = jnp.sum(exchange(gain_part, PLANE), axis=(0, 1))
    return (grad_residual, grad_gain, grad_table)


def on_device(residual, final_gain, table, targets, input_ids, loss_mask, embed_cotangent):
    own, width = residual.shape
    n_plane = lax.axis_size(PLANE)
    shape = jax.ShapeDtypeStruct
    ids = jnp.stack([targets.reshape(n_plane, own).T, input_ids.reshape(n_plane, own).T])
    place = lax.axis_index(PLANE)
    me = jnp.stack([lax.axis_index("section"), place, table.shape[0], own]).astype(jnp.int32)
    lanes = -(-SLOTS * n_plane // LANES) * LANES
    everyone = exchange(jnp.broadcast_to(residual[None], (n_plane, own, width)), PLANE)
    everyone = everyone.reshape(n_plane * own, width)
    slot_rows, codes, most = call(
        plan_body,
        (
            shape((2, 1, lanes), jnp.int32),
            shape((2, own, lanes), jnp.int32),
            shape((1,), jnp.int32),
        ),
        1000,
        1000,
        ids, me,
        in_specs=[VMEM, SMEM],
        out_specs=(VMEM, VMEM, SMEM),
    )
    return lax.cond(
        most[0] < SLOTS,
        compact,
        general,
        everyone, (slot_rows, codes, me), residual, final_gain, table, targets, input_ids, loss_mask,
        embed_cotangent,
    )


def solution(mesh):
    placed = (
        P(PLANE, None),
        P(),
        P(EVERY, None),
        P(),
        P(),
        P(),
        P(PLANE, None),
    )
    return jax.shard_map(
        on_device,
        mesh=mesh,
        in_specs=placed,
        out_specs=(P(PLANE, None), P(), P(EVERY, None)),
        check_vma=False,
    )
```

```python
import math

import jax
import jax.numpy as jnp
from jax import lax
from jax.experimental import pallas as pl
from jax.experimental.pallas import tpu as pltpu
from jax.sharding import PartitionSpec as P

PLANE = ("tensor", "dp")
SECTION = ("z", "core")
CHIPS = ("core", "tensor", "dp")
EVERY = ("z", "core", "tensor", "dp")
LANES = 128
SLOTS = 3
VMEM_LIMIT = 24 * 1024 * 1024
F32 = jnp.float32
BF16 = jnp.bfloat16
VMEM = pl.BlockSpec(memory_space=pltpu.VMEM)
ANY = pl.BlockSpec(memory_space=pl.ANY)
SMEM = pl.BlockSpec(memory_space=pltpu.SMEM)


def exchange(pieces, axes):
    return lax.all_to_all(pieces, axes, 0, 0, tiled=True)


def call(body, outs, flops, moved, *operands, in_specs=None, out_specs=None, scratch=()):
    several = isinstance(outs, tuple)
    return pl.pallas_call(
        body,
        out_shape=outs,
        in_specs=in_specs or [VMEM] * len(operands),
        out_specs=out_specs or ((VMEM,) * len(outs) if several else VMEM),
        scratch_shapes=list(scratch),
        compiler_params=pltpu.CompilerParams(vmem_limit_bytes=VMEM_LIMIT),
        cost_estimate=pl.CostEstimate(flops=flops, bytes_accessed=moved, transcendentals=0),
    )(*operands)


def norm_rows(res_ref, gain_ref, hidden_ref, inverse_ref):
    tokens = res_ref.shape[0]
    step = 16

    def norm(i, carry):
        rows = pl.ds(pl.multiple_of(i * step, step), step)
        x = res_ref[rows, :].astype(F32)
        inverse = 1.0 / jnp.sqrt(jnp.mean(x * x, axis=1, keepdims=True) + 1e-06)
        inverse_ref[rows, :] = jnp.broadcast_to(inverse, (step, LANES))
        hidden_ref[rows, :] = (x * inverse * gain_ref[...]).astype(BF16)
        return carry

    lax.fori_loop(0, tokens // step, norm, 0, unroll=4)


def scores_of(table_ref, hidden_ref):
    scores = lax.dot_general(
        table_ref[...], hidden_ref[...], (((1,), (1,)), ((), ())), preferred_element_type=F32
    )
    return 30.0 * jnp.tanh(scores * (1.0 / 30.0))


def capped_scores(res_ref, gain_ref, table_ref, hidden_ref, inverse_ref):
    norm_rows(res_ref, gain_ref, hidden_ref, inverse_ref)
    return scores_of(table_ref, hidden_ref)


def logit_grads(capped, first_ref, arrived_ref, targets_ref, mask_ref):
    totals = arrived_ref[0]
    for i in range(1, arrived_ref.shape[0]):
        totals = totals + arrived_ref[i]
    rows = lax.broadcasted_iota(jnp.int32, capped.shape, 0)
    hit = (targets_ref[...] - first_ref[0] == rows).astype(F32)
    share = jnp.exp(capped) * (1.0 / totals)
    bend = capped * (1.0 / 30.0)
    return (mask_ref[...].astype(F32) * (share - hit) * (1.0 - bend * bend)).astype(BF16)


def sums_body(res_ref, gain_ref, table_ref, sums_ref, hidden_ref, inverse_ref):
    capped = capped_scores(res_ref, gain_ref, table_ref, hidden_ref, inverse_ref)
    sums = jnp.sum(jnp.exp(capped), axis=0, keepdims=True)
    for i in range(sums_ref.shape[0]):
        sums_ref[i] = sums


def spread_body(in_ref, out_ref):
    total = in_ref[0]
    for i in range(1, in_ref.shape[0]):
        total = total + in_ref[i]
    for i in range(out_ref.shape[0]):
        out_ref[i] = total


def partial_body(
    first_ref, arrived_ref, targets_ref, mask_ref, res_ref, gain_ref, table_ref,
    packed_ref, hidden_ref, inverse_ref, rider_ref,
):
    n_plane, own, packed_width = packed_ref.shape
    width = res_ref.shape[1]
    capped = capped_scores(res_ref, gain_ref, table_ref, hidden_ref, inverse_ref)
    dlogits = logit_grads(capped, first_ref, arrived_ref, targets_ref, mask_ref)
    rider_ref[...] = jnp.zeros_like(rider_ref)
    tile = 2 * LANES
    n_lanes = width // LANES
    inverse = jnp.concatenate([inverse_ref[...]] * 2, axis=1)
    for n in range(width // tile):
        columns = slice(n * tile, (n + 1) * tile)
        part = lax.dot_general(
            dlogits, table_ref[:, columns], (((0,), (0,)), ((), ())), preferred_element_type=F32
        )
        packed_ref[:, :, columns] = part.astype(BF16).reshape(n_plane, own, tile)
        normed = res_ref[:, columns].astype(F32) * inverse
        gain = jnp.sum(part * normed, axis=0, keepdims=True)
        high = gain.astype(BF16).astype(F32)
        low = gain - high
        for k in range(2):
            piece = slice(k * LANES, (k + 1) * LANES)
            rider_ref[2 * n + k : 2 * n + k + 1, :] = high[:, piece]
            rider_ref[n_lanes + 2 * n + k : n_lanes + 2 * n + k + 1, :] = low[:, piece]
    for j in range(rider_ref.shape[0] // own):
        block = rider_ref[j * own : (j + 1) * own, :].astype(BF16)
        for i in range(n_plane):
            packed_ref[i, :, width + j * LANES : width + (j + 1) * LANES] = block


def split_body(in_ref, out_ref, gain_ref):
    n_plane, own, packed_width = in_ref.shape
    n_section = out_ref.shape[0]
    cut = out_ref.shape[2] - LANES
    halves = n_section // own
    width = halves * cut
    n_lanes = width // LANES
    total = in_ref[0].astype(F32)
    for i in range(1, n_plane):
        total = total + in_ref[i].astype(F32)
    for h in range(halves):
        out_ref[h * own : (h + 1) * own, 0, :cut] = total[:, h * cut : (h + 1) * cut]
    for j in range((packed_width - width) // LANES):
        gain_ref[j * own : (j + 1) * own, :] = total[:, width + j * LANES : width + (j + 1) * LANES]
    rows = gain_ref[:n_lanes, :] + gain_ref[n_lanes : 2 * n_lanes, :]
    out_ref[:n_lanes, 0, cut:] = rows
    out_ref[n_lanes:, 0, cut:] = jnp.zeros((n_section - n_lanes, LANES), F32)


def finish_body(in_ref, res_ref, gain_ref, grad_ref, grad_gain_ref):
    n_section = in_ref.shape[0]
    own, width = res_ref.shape
    cut = in_ref.shape[2] - LANES
    halves = n_section // own
    x = res_ref[...].astype(F32)
    inverse = 1.0 / jnp.sqrt(jnp.mean(x * x, axis=1, keepdims=True) + 1e-06)
    normed = x * inverse
    grad_hidden = jnp.concatenate(
        [in_ref[h * own : (h + 1) * own, 0, :cut] for h in range(halves)], axis=1
    )
    scaled = grad_hidden * gain_ref[...]
    along = jnp.mean(scaled * normed, axis=1, keepdims=True)
    grad_ref[...] = ((scaled - normed * along) * inverse).astype(BF16)
    grad_gain_ref[...] = in_ref[: width // LANES, 0, cut:]


def table_body(
    first_ref, arrived_ref, targets_ref, mask_ref, res_ref, gain_ref, table_ref, ids_ref,
    cotangent_ref, out_ref, hidden_ref, inverse_ref,
):
    vocab_rows, width = out_ref.shape
    capped = capped_scores(res_ref, gain_ref, table_ref, hidden_ref, inverse_ref)
    dlogits = logit_grads(capped, first_ref, arrived_ref, targets_ref, mask_ref)
    rows = lax.broadcasted_iota(jnp.int32, capped.shape, 0)
    onehot = (ids_ref[...] - first_ref[0] == rows).astype(F32).astype(BF16)
    scale = math.sqrt(width)
    tile = 2 * LANES
    for n in range(width // tile):
        columns = slice(n * tile, (n + 1) * tile)
        head = jnp.dot(dlogits, hidden_ref[:, columns], preferred_element_type=F32)
        inputs = jnp.dot(onehot, cotangent_ref[:, columns], preferred_element_type=F32)
        out_ref[:, columns] = (head + scale * inputs).astype(BF16)


def plan_body(ids_ref, me_ref, rows_ref, codes_ref, most_ref):
    _, own, groups = ids_ref.shape
    section, place, vocab_rows = me_ref[0], me_ref[1], me_ref[2]
    device = section * groups + place
    most = jnp.int32(0)
    for which in range(2):
        ids = ids_ref[which]
        token = lax.broadcasted_iota(jnp.int32, ids.shape, 0)
        group = lax.broadcasted_iota(jnp.int32, ids.shape, 1)
        owner = lax.div(ids, vocab_rows)
        again = jnp.zeros(ids.shape, jnp.int32)
        for j in range(own):
            again = again + jnp.where((ids == ids[j : j + 1]) & (token > j), 1, 0)
        first = jnp.where(again == 0, 1, 0)
        slot = jnp.zeros(ids.shape, jnp.int32)
        for j in range(own):
            under = (owner == owner[j : j + 1]) & (ids[j : j + 1] < ids) & (first[j : j + 1] == 1)
            slot = slot + jnp.where(under, 1, 0)
        most = jnp.maximum(most, jnp.max(slot))
        rows_ref[which] = jnp.full(rows_ref.shape[1:], -1, jnp.int32)
        mine = (owner == device) & (first == 1)
        for k in range(SLOTS):
            local = jnp.where(mine & (slot == k), ids - device * vocab_rows + 1, 0)
            rows_ref[which, :, k * groups : (k + 1) * groups] = (
                jnp.sum(local, axis=0, keepdims=True) - 1
            )
        near = owner - section * groups
        code = jnp.where((near >= 0) & (near < groups), slot * groups + near, -1)
        code = jnp.sum(jnp.where(group == place, code, 0), axis=1, keepdims=True)
        codes_ref[which] = jnp.broadcast_to(code, codes_ref.shape[1:])
    most_ref[0] = most


def three_terms(x):
    high = x.astype(BF16).astype(F32)
    middle = (x - high).astype(BF16).astype(F32)
    return high, middle, x - high - middle


def slot_layout(own, width, tokens):
    n_lanes = width // LANES
    token_tiles = -(-tokens // LANES)
    scalar_tiles = -(-6 * token_tiles // own)
    slot_tiles = -(-2 * SLOTS * n_lanes // own)
    return n_lanes, token_tiles, scalar_tiles, slot_tiles


def slots_body(table_ref, slot_rows_ref, codes_ref, cotangent_ref, out_ref, room_ref):
    n_plane, own, _ = out_ref.shape
    vocab_rows, width = table_ref.shape
    n_lanes, _, _, tiles = slot_layout(own, width, own * n_plane)
    stride = tiles * own

    def put(at, value):
        room_ref[pl.ds(at, n_plane, stride=stride), :] = value

    for at in range(2 * SLOTS * n_lanes, stride):
        put(at, jnp.zeros((n_plane, LANES), F32))
    n_slots = SLOTS * n_plane
    slot_iota = lax.broadcasted_iota(jnp.int32, (vocab_rows, n_slots), 0)
    pick = (slot_rows_ref[0, :, :n_slots] == slot_iota).astype(F32).astype(BF16)
    own_iota = lax.broadcasted_iota(jnp.int32, (own, n_slots), 1)
    give = (codes_ref[1, :, :n_slots] == own_iota).astype(F32).astype(BF16)
    dims = (((0,), (0,)), ((), ()))
    tile = 2 * LANES
    for n in range(width // tile):
        columns = slice(n * tile, (n + 1) * tile)
        moved = (
            lax.dot_general(pick, table_ref[:, columns], dims, preferred_element_type=F32),
            lax.dot_general(give, cotangent_ref[:, columns], dims, preferred_element_type=F32),
        )
        for which in range(2):
            for k in range(SLOTS):
                block = moved[which][k * n_plane : (k + 1) * n_plane]
                for half in range(2):
                    at = (which * SLOTS + k) * n_lanes + 2 * n + half
                    put(at, block[:, half * LANES : (half + 1) * LANES])
    for p in range(n_plane):
        for t in range(tiles):
            start = p * stride + t * own
            out_ref[p, :, t * LANES : (t + 1) * LANES] = (
                room_ref[start : start + own, :].astype(BF16)
            )


def compact_body(
    res_hbm, table_hbm, slots_hbm, gain_ref, target_row_ref, mask_ref,
    packed_ref, res_ref, table_ref, slots_ref, hidden_ref, inverse_ref, tokens_ref, room_ref, sems,
):
    copies = [
        pltpu.make_async_copy(res_hbm, res_ref, sems.at[0]),
        pltpu.make_async_copy(table_hbm, table_ref, sems.at[1]),
        pltpu.make_async_copy(slots_hbm, slots_ref, sems.at[2]),
    ]
    for copy in copies:
        copy.start()
    n_plane, own, packed_width = packed_ref.shape
    tokens, width = res_ref.shape
    n_lanes, token_tiles, scalar_tiles, _ = slot_layout(own, width, tokens)
    copies[0].wait()
    norm_rows(res_ref, gain_ref, hidden_ref, inverse_ref)
    copies[1].wait()
    capped = scores_of(table_ref, hidden_ref)
    rows = lax.broadcasted_iota(jnp.int32, capped.shape, 0)
    hit = target_row_ref[...] == rows
    expterm = jnp.exp(capped)
    bend = capped * (1.0 / 30.0)
    weight = mask_ref[...].astype(F32) * (1.0 - bend * bend)
    unscaled = jnp.where(hit, 0.0, weight * expterm).astype(BF16)
    pieces = [
        jnp.sum(expterm, axis=0, keepdims=True),
        jnp.sum(jnp.where(hit, capped, 0.0), axis=0, keepdims=True),
    ]
    tokens_ref[...] = jnp.zeros_like(tokens_ref)
    room_ref[...] = jnp.zeros_like(room_ref)
    for which in range(2):
        for term, value in enumerate(three_terms(pieces[which])):
            tokens_ref[:, :tokens] = value
            for t in range(token_tiles):
                at = (which * 3 + term) * token_tiles + t
                room_ref[at : at + 1, :] = tokens_ref[:, t * LANES : (t + 1) * LANES]
    for t in range(scalar_tiles):
        block = room_ref[t * own : (t + 1) * own, :].astype(BF16)
        for p in range(n_plane):
            packed_ref[p, :, width + t * LANES : width + (t + 1) * LANES] = block
    tile = 2 * LANES
    for n in range(width // tile):
        columns = slice(n * tile, (n + 1) * tile)
        part = lax.dot_general(
            unscaled, table_ref[:, columns], (((0,), (0,)), ((), ())), preferred_element_type=F32
        )
        packed_ref[:, :, columns] = part.astype(BF16).reshape(n_plane, own, tile)
    copies[2].wait()
    packed_ref[:, :, width + scalar_tiles * LANES :] = slots_ref[...]


def unpack_body(
    in_ref, place_ref, codes_ref, out_ref, rows_out_ref, room_ref, moved_ref, rest_ref
):
    n_plane, own, packed_width = in_ref.shape
    tokens = n_plane * own
    n_section = out_ref.shape[0]
    halves = n_section // own
    width = rows_out_ref.shape[1]
    cut = width // halves
    n_lanes, token_tiles, scalar_tiles, slot_tiles = slot_layout(own, width, tokens)
    tiles = scalar_tiles + slot_tiles
    stride = tiles * own
    total = in_ref[0, :, :width].astype(F32)
    for p in range(1, n_plane):
        total = total + in_ref[p, :, :width].astype(F32)
    for p in range(n_plane):
        for t in range(tiles):
            start = p * stride + t * own
            room_ref[start : start + own, :] = in_ref[
                p, :, width + t * LANES : width + (t + 1) * LANES
            ].astype(F32)

    def take(at):
        return room_ref[pl.ds(at, n_plane, stride=stride), :]

    for which in range(2):
        for k in range(SLOTS):
            for j in range(n_lanes):
                moved_ref[
                    which, k * n_plane : (k + 1) * n_plane, j * LANES : (j + 1) * LANES
                ] = take(scalar_tiles * own + (which * SLOTS + k) * n_lanes + j)
    rows_out_ref[...] = moved_ref[1].astype(BF16)
    n_slots = SLOTS * n_plane
    own_iota = lax.broadcasted_iota(jnp.int32, (own, n_slots), 1)
    choose = (codes_ref[0, :, :n_slots] == own_iota).astype(F32).astype(BF16)
    target_rows = jnp.dot(choose, moved_ref[0].astype(BF16), preferred_element_type=F32)
    for h in range(halves):
        for i in range(own):
            s = i * halves + h
            rest_ref[2 * s : 2 * s + 1, :cut] = total[i : i + 1, h * cut : (h + 1) * cut]
            rest_ref[2 * s + 1 : 2 * s + 2, :cut] = target_rows[i : i + 1, h * cut : (h + 1) * cut]

    def summed(which):
        tiles_of = []
        for t in range(token_tiles):
            terms = [
                jnp.sum(take((which * 3 + term) * token_tiles + t), axis=0, keepdims=True)
                for term in range(3)
            ]
            tiles_of.append(terms[0] + terms[1] + terms[2])
        return tiles_of

    lane = lax.broadcasted_iota(jnp.int32, (own, LANES), 1)
    token = lax.broadcasted_iota(jnp.int32, (own, LANES), 0) + place_ref[0] * own
    score = jnp.zeros((own, 1), F32)
    for t, value in enumerate(summed(1)):
        score = score + jnp.sum(
            jnp.where(lane + t * LANES == token, jnp.broadcast_to(value, lane.shape), 0.0),
            axis=1,
            keepdims=True,
        )
    high, middle, low = three_terms(score)
    scores = jnp.where(lane == 0, high, jnp.where(lane == 1, middle, jnp.where(lane == 2, low, 0.0)))
    sums = [three_terms(value) for value in summed(0)]
    extra = [sums[t][term] for term in range(3) for t in range(token_tiles)]
    per_row = (len(extra) + 2) // 2
    for s in range(n_section):
        i = s // halves
        for n, value in enumerate(extra + [scores[i : i + 1]]):
            row, column = 2 * s + n // per_row, cut + n % per_row * LANES
            rest_ref[row : row + 1, column : column + LANES] = value
        for n in range(len(extra) + 1, 2 * per_row):
            row, column = 2 * s + n // per_row, cut + n % per_row * LANES
            rest_ref[row : row + 1, column : column + LANES] = jnp.zeros((1, LANES), F32)
    for s in range(n_section):
        out_ref[s] = rest_ref[2 * s : 2 * s + 2, :].astype(BF16)


def combine_body(in_ref, me_ref, mask_ref, out_ref, totals_ref, tokens_ref):
    n_section, _, piece_width = in_ref.shape
    cut = out_ref.shape[2]
    tokens = totals_ref.shape[1]
    own = out_ref.shape[0]
    halves = n_section // own
    total = in_ref[0].astype(F32)
    for s in range(1, n_section):
        total = total + in_ref[s].astype(F32)
    token_tiles = -(-tokens // LANES)
    per_row = (piece_width - cut) // LANES

    def tile_of(n):
        row, column = n // per_row, cut + n % per_row * LANES
        return total[row : row + 1, column : column + LANES]

    for t in range(token_tiles):
        tokens_ref[:, t * LANES : (t + 1) * LANES] = (
            tile_of(t) + tile_of(token_tiles + t) + tile_of(2 * token_tiles + t)
        )
    totals = tokens_ref[:, :tokens]
    totals_ref[...] = totals
    token = me_ref[1] * own + lax.div(me_ref[0], halves)
    here = lax.broadcasted_iota(jnp.int32, totals.shape, 1) == token
    whole = jnp.sum(jnp.where(here, totals, 0.0), axis=1, keepdims=True)
    weight = jnp.sum(jnp.where(here, mask_ref[...].astype(F32), 0.0), axis=1, keepdims=True)
    score = jnp.sum(tile_of(3 * token_tiles), axis=1, keepdims=True)
    bend = score * (1.0 / 30.0)
    at_target = weight * (jnp.exp(score) / whole - 1.0) * (1.0 - bend * bend)
    at_target = at_target.astype(BF16).astype(F32)
    grad = total[0:1, :cut] / whole + at_target * total[1:2, :cut]
    for s in range(out_ref.shape[0]):
        out_ref[s] = grad


def normed_rows(res_ref):
    x = res_ref[...].astype(F32)
    inverse = 1.0 / jnp.sqrt(jnp.mean(x * x, axis=1, keepdims=True) + 1e-06)
    return x * inverse, inverse


def gain_body(in_ref, core_ref, res_ref, out_ref):
    own, _, cut = in_ref.shape
    normed, _ = normed_rows(res_ref)
    half = jnp.where(core_ref[0] == 0, normed[:, :cut], normed[:, cut:])
    gain = jnp.sum(in_ref[:, 0, :] * half, axis=0, keepdims=True)
    for i in range(out_ref.shape[0]):
        out_ref[i] = gain


def close_body(in_ref, other_ref, core_ref, res_ref, gain_ref, grad_ref):
    mine, other = in_ref[:, 0, :], other_ref[:, 0, :]
    at_left = core_ref[0] == 0
    left, right = jnp.where(at_left, mine, other), jnp.where(at_left, other, mine)
    normed, inverse = normed_rows(res_ref)
    scaled = jnp.concatenate([left, right], axis=1) * gain_ref[...]
    along = jnp.mean(scaled * normed, axis=1, keepdims=True)
    grad_ref[...] = ((scaled - normed * along) * inverse).astype(BF16)


def compact_table_body(
    target_row_ref, totals_ref, mask_ref, res_ref, gain_ref, table_ref, slot_rows_ref, moved_ref,
    out_ref, hidden_ref, inverse_ref,
):
    vocab_rows, width = out_ref.shape
    capped = capped_scores(res_ref, gain_ref, table_ref, hidden_ref, inverse_ref)
    rows = lax.broadcasted_iota(jnp.int32, capped.shape, 0)
    hit = (target_row_ref[...] == rows).astype(F32)
    share = jnp.exp(capped) * (1.0 / totals_ref[...])
    bend = capped * (1.0 / 30.0)
    dlogits = (mask_ref[...].astype(F32) * (share - hit) * (1.0 - bend * bend)).astype(BF16)
    n_slots = moved_ref.shape[0]
    slot_iota = lax.broadcasted_iota(jnp.int32, (vocab_rows, n_slots), 0)
    onehot = (slot_rows_ref[1, :, :n_slots] == slot_iota).astype(F32).astype(BF16)
    scale = math.sqrt(width)
    tile = 2 * LANES
    for n in range(width // tile):
        columns = slice(n * tile, (n + 1) * tile)
        head = jnp.dot(dlogits, hidden_ref[:, columns], preferred_element_type=F32)
        inputs = jnp.dot(onehot, moved_ref[:, columns], preferred_element_type=F32)
        out_ref[:, columns] = (head + scale * inputs).astype(BF16)


def general(
    everyone, plan, residual, final_gain, table, targets, input_ids, loss_mask, embed_cotangent
):
    del plan
    own, width = residual.shape
    vocab_rows = table.shape[0]
    n_plane, n_section = lax.axis_size(PLANE), lax.axis_size(SECTION)
    tokens = own * n_plane
    cut = own * width // n_section
    n_lanes = width // LANES
    rider = -(-2 * n_lanes // own) * own
    product = 2 * tokens * vocab_rows * width
    shape = jax.ShapeDtypeStruct
    first = (lax.axis_index(EVERY) * vocab_rows).astype(jnp.int32).reshape(1)
    gain_row = final_gain.reshape(1, width)

    packed_width = width + rider // own * LANES
    norm_rooms = [pltpu.VMEM((tokens, width), BF16), pltpu.VMEM((tokens, LANES), F32)]
    rows_bytes = vocab_rows * width * 2

    wide = jnp.pad(embed_cotangent, ((0, 0), (0, 512)))
    all_cotangent = lax.all_gather(wide, PLANE, axis=0, tiled=True)

    sums = call(
        sums_body,
        shape((n_section, 1, tokens), F32),
        product,
        rows_bytes,
        everyone, gain_row, table,
        scratch=norm_rooms,
    )
    sums = call(
        spread_body, shape((n_plane, 1, tokens), F32), tokens, 4 * tokens, exchange(sums, SECTION)
    )
    given = (
        first, exchange(sums, PLANE), targets.reshape(1, tokens), loss_mask.reshape(1, tokens),
        everyone, gain_row, table,
    )
    packed = call(
        partial_body,
        shape((n_plane, own, packed_width), BF16),
        2 * product,
        rows_bytes,
        *given,
        in_specs=[SMEM] + [VMEM] * 6,
        scratch=norm_rooms + [pltpu.VMEM((rider, LANES), F32)],
    )
    arrived = exchange(packed, PLANE)
    split = call(
        split_body,
        shape((n_section, 1, cut + LANES), F32),
        tokens * width,
        tokens * width * 2,
        arrived,
        scratch=[pltpu.VMEM((rider, LANES), F32)],
    )
    reduced = call(
        spread_body,
        shape((n_section, 1, cut + LANES), F32),
        own * width,
        own * width * 8,
        exchange(split, SECTION),
    )
    grad_table = call(
        table_body,
        shape((vocab_rows, width), BF16),
        3 * product,
        2 * rows_bytes,
        *given, input_ids.reshape(1, tokens), all_cotangent,
        in_specs=[SMEM] + [VMEM] * 8,
        scratch=norm_rooms,
    )
    summed, grad_table = lax.optimization_barrier((exchange(reduced, SECTION), grad_table))
    grad_residual, grad_gain = call(
        finish_body,
        (shape((own, width), BF16), shape((n_lanes, LANES), F32)),
        own * width * 10,
        own * width * 8,
        summed, residual, gain_row,
    )
    return (grad_residual, grad_gain.reshape(width), grad_table)


def compact(
    everyone, plan, residual, final_gain, table, targets, input_ids, loss_mask, embed_cotangent
):
    del input_ids, embed_cotangent
    slot_rows, codes, slots, me = plan
    own, width = residual.shape
    vocab_rows = table.shape[0]
    n_plane, n_section = lax.axis_size(PLANE), lax.axis_size(SECTION)
    tokens = own * n_plane
    cut = own * width // n_section
    product = 2 * tokens * vocab_rows * width
    rows_bytes = vocab_rows * width * 2
    shape = jax.ShapeDtypeStruct
    _, token_tiles, scalar_tiles, slot_tiles = slot_layout(own, width, tokens)
    tiles = scalar_tiles + slot_tiles
    packed_width = width + tiles * LANES
    piece_width = cut + (3 * token_tiles + 2) // 2 * LANES
    norm_rooms = [pltpu.VMEM((tokens, width), BF16), pltpu.VMEM((tokens, LANES), F32)]
    gain_row = final_gain.reshape(1, width)
    mask = loss_mask.reshape(1, tokens)
    target_row = targets.reshape(1, tokens) - (me[0] * n_plane + me[1]) * vocab_rows

    packed = call(
        compact_body,
        shape((n_plane, own, packed_width), BF16),
        2 * product,
        rows_bytes,
        everyone, table, slots, gain_row, target_row, mask,
        in_specs=[ANY] * 3 + [VMEM] * 3,
        scratch=[
            pltpu.VMEM((tokens, width), BF16),
            pltpu.VMEM((vocab_rows, width), BF16),
            pltpu.VMEM((n_plane, own, slot_tiles * LANES), BF16),
        ] + norm_rooms + [
            pltpu.VMEM((1, token_tiles * LANES), F32),
            pltpu.VMEM((scalar_tiles * own, LANES), F32),
            pltpu.SemaphoreType.DMA((3,)),
        ],
    )
    pieces, moved = call(
        unpack_body,
        (
            shape((n_section, 2, piece_width), BF16),
            shape((SLOTS * n_plane, width), BF16),
        ),
        tokens * width,
        tokens * packed_width * 2,
        exchange(packed, PLANE), me[1:2], codes,
        in_specs=[VMEM, SMEM, VMEM],
        scratch=[
            pltpu.VMEM((n_plane * tiles * own, LANES), F32),
            pltpu.VMEM((2, SLOTS * n_plane, width), F32),
            pltpu.VMEM((2 * n_section, piece_width), F32),
        ],
    )
    half_token, totals = call(
        combine_body,
        (shape((own, 1, cut), F32), shape((1, tokens), F32)),
        own * width,
        own * width * 8,
        exchange(pieces, SECTION), me, mask,
        in_specs=[VMEM, SMEM, VMEM],
        scratch=[pltpu.VMEM((1, token_tiles * LANES), F32)],
    )
    grad_table = call(
        compact_table_body,
        shape((vocab_rows, width), BF16),
        3 * product,
        2 * rows_bytes,
        target_row, totals, mask, everyone, gain_row, table, slot_rows, moved,
        scratch=norm_rooms,
    )
    mine, grad_table = lax.optimization_barrier((exchange(half_token, "z"), grad_table))
    core = lax.axis_index("core").astype(jnp.int32).reshape(1)
    n_chips = lax.axis_size(CHIPS)
    other = lax.ppermute(mine, "core", [(0, 1), (1, 0)])
    gain_part = call(
        gain_body,
        shape((n_chips, 1, cut), F32),
        own * width * 4,
        own * width * 8,
        mine, core, residual,
        in_specs=[VMEM, SMEM, VMEM],
    )
    grad_residual = call(
        close_body,
        shape((own, width), BF16),
        own * width * 10,
        own * width * 8,
        mine, other, core, residual, gain_row,
        in_specs=[VMEM, VMEM, SMEM, VMEM, VMEM],
    )
    grad_gain = exchange(gain_part, CHIPS).reshape(n_chips // n_plane, n_plane, cut)
    return (grad_residual, jnp.sum(grad_gain, axis=1).reshape(width), grad_table)


def on_device(residual, final_gain, table, targets, input_ids, loss_mask, embed_cotangent):
    own, width = residual.shape
    n_plane = lax.axis_size(PLANE)
    shape = jax.ShapeDtypeStruct
    ids = jnp.stack([targets.reshape(n_plane, own).T, input_ids.reshape(n_plane, own).T])
    place = lax.axis_index(PLANE)
    me = jnp.stack([lax.axis_index(SECTION), place, table.shape[0], own]).astype(jnp.int32)
    lanes = -(-SLOTS * n_plane // LANES) * LANES
    everyone = exchange(jnp.broadcast_to(residual[None], (n_plane, own, width)), PLANE)
    everyone = everyone.reshape(n_plane * own, width)
    slot_rows, codes, most = call(
        plan_body,
        (
            shape((2, 1, lanes), jnp.int32),
            shape((2, own, lanes), jnp.int32),
            shape((1,), jnp.int32),
        ),
        1000,
        1000,
        ids, me,
        in_specs=[VMEM, SMEM],
        out_specs=(VMEM, VMEM, SMEM),
    )
    slot_tiles = slot_layout(own, width, own * n_plane)[3]
    slots = call(
        slots_body,
        shape((n_plane, own, slot_tiles * LANES), BF16),
        1000,
        1000,
        table, slot_rows, codes, embed_cotangent,
        scratch=[pltpu.VMEM((n_plane * slot_tiles * own, LANES), F32)],
    )
    return lax.cond(
        most[0] < SLOTS,
        compact,
        general,
        everyone, (slot_rows, codes, slots, me), residual, final_gain, table, targets, input_ids, loss_mask,
        embed_cotangent,
    )


def solution(mesh):
    cores = 2
    devices = mesh.devices.reshape(-1, cores, *mesh.devices.shape[1:])
    fine = jax.sharding.Mesh(devices, EVERY)
    placed = (
        P(PLANE, None),
        P(),
        P(EVERY, None),
        P(),
        P(),
        P(),
        P(PLANE, None),
    )
    return jax.shard_map(
        on_device,
        mesh=fine,
        in_specs=placed,
        out_specs=(P(PLANE, None), P(), P(EVERY, None)),
        check_vma=False,
    )
```

```python
import math

import jax
import jax.numpy as jnp
from jax import lax
from jax.experimental import pallas as pl
from jax.experimental.pallas import tpu as pltpu
from jax.sharding import PartitionSpec as P

PLANE = ("tensor", "dp")
SECTION = ("z", "core")
CHIPS = ("core", "tensor", "dp")
EVERY = ("z", "core", "tensor", "dp")
LANES = 128
SLOTS = 3
VMEM_LIMIT = 24 * 1024 * 1024
F32 = jnp.float32
BF16 = jnp.bfloat16
VMEM = pl.BlockSpec(memory_space=pltpu.VMEM)
ANY = pl.BlockSpec(memory_space=pl.ANY)
SMEM = pl.BlockSpec(memory_space=pltpu.SMEM)


def exchange(pieces, axes):
    return lax.all_to_all(pieces, axes, 0, 0, tiled=True)


def call(body, outs, flops, moved, *operands, in_specs=None, out_specs=None, scratch=()):
    several = isinstance(outs, tuple)
    return pl.pallas_call(
        body,
        out_shape=outs,
        in_specs=in_specs or [VMEM] * len(operands),
        out_specs=out_specs or ((VMEM,) * len(outs) if several else VMEM),
        scratch_shapes=list(scratch),
        compiler_params=pltpu.CompilerParams(vmem_limit_bytes=VMEM_LIMIT),
        cost_estimate=pl.CostEstimate(flops=flops, bytes_accessed=moved, transcendentals=0),
    )(*operands)


def norm_rows(res_ref, gain_ref, hidden_ref, inverse_ref):
    tokens = res_ref.shape[0]
    step = 16

    def norm(i, carry):
        rows = pl.ds(pl.multiple_of(i * step, step), step)
        x = res_ref[rows, :].astype(F32)
        inverse = 1.0 / jnp.sqrt(jnp.mean(x * x, axis=1, keepdims=True) + 1e-06)
        inverse_ref[rows, :] = jnp.broadcast_to(inverse, (step, LANES))
        hidden_ref[rows, :] = (x * inverse * gain_ref[...]).astype(BF16)
        return carry

    lax.fori_loop(0, tokens // step, norm, 0, unroll=16)


def scores_of(table_ref, hidden_ref):
    vocab_rows, block = table_ref.shape[0], 256
    scores = [
        lax.dot_general(
            table_ref[start : min(start + block, vocab_rows), :],
            hidden_ref[...],
            (((1,), (1,)), ((), ())),
            preferred_element_type=F32,
        )
        for start in range(0, vocab_rows, block)
    ]
    scores = jnp.concatenate(scores, axis=0)
    return 30.0 * jnp.tanh(scores * (1.0 / 30.0))


def capped_scores(res_ref, gain_ref, table_ref, hidden_ref, inverse_ref):
    norm_rows(res_ref, gain_ref, hidden_ref, inverse_ref)
    return scores_of(table_ref, hidden_ref)


def logit_grads(capped, first_ref, arrived_ref, targets_ref, mask_ref):
    totals = arrived_ref[0]
    for i in range(1, arrived_ref.shape[0]):
        totals = totals + arrived_ref[i]
    rows = lax.broadcasted_iota(jnp.int32, capped.shape, 0)
    hit = (targets_ref[...] - first_ref[0] == rows).astype(F32)
    share = jnp.exp(capped) * (1.0 / totals)
    bend = capped * (1.0 / 30.0)
    return (mask_ref[...].astype(F32) * (share - hit) * (1.0 - bend * bend)).astype(BF16)


def sums_body(res_ref, gain_ref, table_ref, sums_ref, hidden_ref, inverse_ref):
    capped = capped_scores(res_ref, gain_ref, table_ref, hidden_ref, inverse_ref)
    sums = jnp.sum(jnp.exp(capped), axis=0, keepdims=True)
    for i in range(sums_ref.shape[0]):
        sums_ref[i] = sums


def spread_body(in_ref, out_ref):
    total = in_ref[0]
    for i in range(1, in_ref.shape[0]):
        total = total + in_ref[i]
    for i in range(out_ref.shape[0]):
        out_ref[i] = total


def partial_body(
    first_ref, arrived_ref, targets_ref, mask_ref, res_ref, gain_ref, table_ref,
    packed_ref, hidden_ref, inverse_ref, rider_ref,
):
    n_plane, own, packed_width = packed_ref.shape
    width = res_ref.shape[1]
    capped = capped_scores(res_ref, gain_ref, table_ref, hidden_ref, inverse_ref)
    dlogits = logit_grads(capped, first_ref, arrived_ref, targets_ref, mask_ref)
    rider_ref[...] = jnp.zeros_like(rider_ref)
    tile = 2 * LANES
    n_lanes = width // LANES
    inverse = jnp.concatenate([inverse_ref[...]] * 2, axis=1)
    for n in range(width // tile):
        columns = slice(n * tile, (n + 1) * tile)
        part = lax.dot_general(
            dlogits, table_ref[:, columns], (((0,), (0,)), ((), ())), preferred_element_type=F32
        )
        packed_ref[:, :, columns] = part.astype(BF16).reshape(n_plane, own, tile)
        normed = res_ref[:, columns].astype(F32) * inverse
        gain = jnp.sum(part * normed, axis=0, keepdims=True)
        high = gain.astype(BF16).astype(F32)
        low = gain - high
        for k in range(2):
            piece = slice(k * LANES, (k + 1) * LANES)
            rider_ref[2 * n + k : 2 * n + k + 1, :] = high[:, piece]
            rider_ref[n_lanes + 2 * n + k : n_lanes + 2 * n + k + 1, :] = low[:, piece]
    for j in range(rider_ref.shape[0] // own):
        block = rider_ref[j * own : (j + 1) * own, :].astype(BF16)
        for i in range(n_plane):
            packed_ref[i, :, width + j * LANES : width + (j + 1) * LANES] = block


def split_body(in_ref, out_ref, gain_ref):
    n_plane, own, packed_width = in_ref.shape
    n_section = out_ref.shape[0]
    cut = out_ref.shape[2] - LANES
    halves = n_section // own
    width = halves * cut
    n_lanes = width // LANES
    total = in_ref[0].astype(F32)
    for i in range(1, n_plane):
        total = total + in_ref[i].astype(F32)
    for h in range(halves):
        out_ref[h * own : (h + 1) * own, 0, :cut] = total[:, h * cut : (h + 1) * cut]
    for j in range((packed_width - width) // LANES):
        gain_ref[j * own : (j + 1) * own, :] = total[:, width + j * LANES : width + (j + 1) * LANES]
    rows = gain_ref[:n_lanes, :] + gain_ref[n_lanes : 2 * n_lanes, :]
    out_ref[:n_lanes, 0, cut:] = rows
    out_ref[n_lanes:, 0, cut:] = jnp.zeros((n_section - n_lanes, LANES), F32)


def finish_body(in_ref, res_ref, gain_ref, grad_ref, grad_gain_ref):
    n_section = in_ref.shape[0]
    own, width = res_ref.shape
    cut = in_ref.shape[2] - LANES
    halves = n_section // own
    x = res_ref[...].astype(F32)
    inverse = 1.0 / jnp.sqrt(jnp.mean(x * x, axis=1, keepdims=True) + 1e-06)
    normed = x * inverse
    grad_hidden = jnp.concatenate(
        [in_ref[h * own : (h + 1) * own, 0, :cut] for h in range(halves)], axis=1
    )
    scaled = grad_hidden * gain_ref[...]
    along = jnp.mean(scaled * normed, axis=1, keepdims=True)
    grad_ref[...] = ((scaled - normed * along) * inverse).astype(BF16)
    grad_gain_ref[...] = in_ref[: width // LANES, 0, cut:]


def table_body(
    first_ref, arrived_ref, targets_ref, mask_ref, res_ref, gain_ref, table_ref, ids_ref,
    cotangent_ref, out_ref, hidden_ref, inverse_ref,
):
    vocab_rows, width = out_ref.shape
    capped = capped_scores(res_ref, gain_ref, table_ref, hidden_ref, inverse_ref)
    dlogits = logit_grads(capped, first_ref, arrived_ref, targets_ref, mask_ref)
    rows = lax.broadcasted_iota(jnp.int32, capped.shape, 0)
    onehot = (ids_ref[...] - first_ref[0] == rows).astype(F32).astype(BF16)
    scale = math.sqrt(width)
    tile = 2 * LANES
    for n in range(width // tile):
        columns = slice(n * tile, (n + 1) * tile)
        head = jnp.dot(dlogits, hidden_ref[:, columns], preferred_element_type=F32)
        inputs = jnp.dot(onehot, cotangent_ref[:, columns], preferred_element_type=F32)
        out_ref[:, columns] = (head + scale * inputs).astype(BF16)


def plan_body(ids_ref, me_ref, rows_ref, codes_ref, pairs_ref):
    _, own, groups = ids_ref.shape
    section, place, vocab_rows = me_ref[0], me_ref[1], me_ref[2]
    device = section * groups + place
    token = lax.broadcasted_iota(jnp.int32, (own, groups), 0)
    group = lax.broadcasted_iota(jnp.int32, (own, groups), 1)

    def column(x):
        return jnp.sum(jnp.where(group == place, x, 0), axis=1, keepdims=True)

    ahead_sent = ahead_here = jnp.zeros((1, groups), jnp.int32)
    for which in range(2):
        ids = ids_ref[which]
        owner = lax.div(ids, vocab_rows)
        again = jnp.zeros(ids.shape, jnp.int32)
        for j in range(own):
            again = again + jnp.where((ids == ids[j : j + 1]) & (token > j), 1, 0)
        first = jnp.where(again == 0, 1, 0)
        slot = jnp.zeros(ids.shape, jnp.int32)
        for j in range(own):
            under = (owner == owner[j : j + 1]) & (ids[j : j + 1] < ids) & (first[j : j + 1] == 1)
            slot = slot + jnp.where(under, 1, 0)
        near = column(owner) - section * groups
        inside = (near >= 0) & (near < groups)
        mine = (owner == device) & (first == 1)
        if which == 0:
            offset = jnp.zeros((own, 1), jnp.int32)
            pair = owner * groups + group
        else:
            offset = jnp.sum(jnp.where(group == near, ahead_sent, 0), axis=1, keepdims=True)
            slot_here = slot + ahead_here
            over = lax.div(owner, groups) * groups
            pair = (over + group) * groups + owner - over
        pairs_ref[which] = jnp.where(first == 1, pair, -1)
        code = jnp.where(inside, (column(slot) + offset) * groups + near, -1)
        codes_ref[which] = jnp.broadcast_to(code, codes_ref.shape[1:])
        rows_ref[which] = jnp.full(rows_ref.shape[1:], -1, jnp.int32)
        for k in range(SLOTS):
            taken = mine & ((slot if which == 0 else slot_here) == k)
            local = jnp.where(taken, ids - device * vocab_rows + 1, 0)
            rows_ref[which, :, k * groups : (k + 1) * groups] = (
                jnp.sum(local, axis=0, keepdims=True) - 1
            )
        if which == 0:
            ahead_sent = jnp.sum(jnp.where(mine, 1, 0), axis=0, keepdims=True)
            come = (group == near) & (column(first) == 1)
            ahead_here = jnp.sum(jnp.where(come, 1, 0), axis=0, keepdims=True)


def three_terms(x):
    high = x.astype(BF16).astype(F32)
    middle = (x - high).astype(BF16).astype(F32)
    return high, middle, x - high - middle


def slot_layout(own, width, tokens):
    n_lanes = width // LANES
    token_tiles = -(-tokens // LANES)
    scalar_tiles = -(-6 * token_tiles // own)
    slot_tiles = -(-SLOTS * n_lanes // own)
    return n_lanes, token_tiles, scalar_tiles, slot_tiles


def slots_body(table_ref, slot_rows_ref, codes_ref, cotangent_ref, out_ref, room_ref):
    n_plane, own, _ = out_ref.shape
    vocab_rows, width = table_ref.shape
    n_lanes, _, _, tiles = slot_layout(own, width, own * n_plane)
    stride = tiles * own

    def put(at, value):
        room_ref[pl.ds(at, n_plane, stride=stride), :] = value

    for at in range(SLOTS * n_lanes, stride):
        put(at, jnp.zeros((n_plane, LANES), F32))
    n_slots = SLOTS * n_plane
    slot_iota = lax.broadcasted_iota(jnp.int32, (vocab_rows, n_slots), 0)
    pick = (slot_rows_ref[0, :, :n_slots] == slot_iota).astype(F32).astype(BF16)
    own_iota = lax.broadcasted_iota(jnp.int32, (own, n_slots), 1)
    give = (codes_ref[1, :, :n_slots] == own_iota).astype(F32).astype(BF16)
    dims = (((0,), (0,)), ((), ()))
    tile = 2 * LANES
    for n in range(width // tile):
        columns = slice(n * tile, (n + 1) * tile)
        moved = lax.dot_general(pick, table_ref[:, columns], dims, preferred_element_type=F32)
        moved = moved + lax.dot_general(
            give, cotangent_ref[:, columns], dims, preferred_element_type=F32
        )
        for k in range(SLOTS):
            block = moved[k * n_plane : (k + 1) * n_plane]
            for half in range(2):
                put(k * n_lanes + 2 * n + half, block[:, half * LANES : (half + 1) * LANES])
    for p in range(n_plane):
        for t in range(tiles):
            start = p * stride + t * own
            out_ref[p, :, t * LANES : (t + 1) * LANES] = (
                room_ref[start : start + own, :].astype(BF16)
            )


def compact_body(
    res_hbm, table_hbm, slots_hbm, gain_ref, target_row_ref, mask_ref,
    packed_ref, res_ref, table_ref, slots_ref, hidden_ref, inverse_ref, tokens_ref, room_ref, sems,
):
    copies = [
        pltpu.make_async_copy(res_hbm, res_ref, sems.at[0]),
        pltpu.make_async_copy(table_hbm, table_ref, sems.at[1]),
        pltpu.make_async_copy(slots_hbm, slots_ref, sems.at[2]),
    ]
    for copy in copies:
        copy.start()
    n_plane, own, packed_width = packed_ref.shape
    tokens, width = res_ref.shape
    n_lanes, token_tiles, scalar_tiles, _ = slot_layout(own, width, tokens)
    copies[0].wait()
    norm_rows(res_ref, gain_ref, hidden_ref, inverse_ref)
    copies[1].wait()
    capped = scores_of(table_ref, hidden_ref)
    rows = lax.broadcasted_iota(jnp.int32, capped.shape, 0)
    hit = target_row_ref[...] == rows
    expterm = jnp.exp(capped)
    bend = capped * (1.0 / 30.0)
    weight = mask_ref[...].astype(F32) * (1.0 - bend * bend)
    unscaled = jnp.where(hit, 0.0, weight * expterm).astype(BF16)
    pieces = [
        jnp.sum(expterm, axis=0, keepdims=True),
        jnp.sum(jnp.where(hit, capped, 0.0), axis=0, keepdims=True),
    ]
    tokens_ref[...] = jnp.zeros_like(tokens_ref)
    room_ref[...] = jnp.zeros_like(room_ref)
    for which in range(2):
        for term, value in enumerate(three_terms(pieces[which])):
            tokens_ref[:, :tokens] = value
            for t in range(token_tiles):
                at = (which * 3 + term) * token_tiles + t
                room_ref[at : at + 1, :] = tokens_ref[:, t * LANES : (t + 1) * LANES]
    for t in range(scalar_tiles):
        block = room_ref[t * own : (t + 1) * own, :].astype(BF16)
        for p in range(n_plane):
            packed_ref[p, :, width + t * LANES : width + (t + 1) * LANES] = block
    tile = 2 * LANES
    for n in range(width // tile):
        columns = slice(n * tile, (n + 1) * tile)
        part = lax.dot_general(
            unscaled, table_ref[:, columns], (((0,), (0,)), ((), ())), preferred_element_type=F32
        )
        packed_ref[:, :, columns] = part.astype(BF16).reshape(n_plane, own, tile)
    copies[2].wait()
    packed_ref[:, :, width + scalar_tiles * LANES :] = slots_ref[...]


def unpack_body(
    in_ref, place_ref, codes_ref, out_ref, rows_out_ref, room_ref, moved_ref, rest_ref
):
    n_plane, own, packed_width = in_ref.shape
    tokens = n_plane * own
    n_section = out_ref.shape[0]
    halves = n_section // own
    width = rows_out_ref.shape[1]
    cut = width // halves
    n_lanes, token_tiles, scalar_tiles, slot_tiles = slot_layout(own, width, tokens)
    tiles = scalar_tiles + slot_tiles
    stride = tiles * own
    total = in_ref[0, :, :width].astype(F32)
    for p in range(1, n_plane):
        total = total + in_ref[p, :, :width].astype(F32)
    for p in range(n_plane):
        for t in range(tiles):
            start = p * stride + t * own
            room_ref[start : start + own, :] = in_ref[
                p, :, width + t * LANES : width + (t + 1) * LANES
            ].astype(F32)

    def take(at):
        return room_ref[pl.ds(at, n_plane, stride=stride), :]

    for k in range(SLOTS):
        for j in range(n_lanes):
            moved_ref[k * n_plane : (k + 1) * n_plane, j * LANES : (j + 1) * LANES] = take(
                scalar_tiles * own + k * n_lanes + j
            )
    moved = moved_ref[...].astype(BF16)
    rows_out_ref[...] = moved
    n_slots = SLOTS * n_plane
    own_iota = lax.broadcasted_iota(jnp.int32, (own, n_slots), 1)
    choose = (codes_ref[0, :, :n_slots] == own_iota).astype(F32).astype(BF16)
    target_rows = jnp.dot(choose, moved, preferred_element_type=F32)
    for h in range(halves):
        for i in range(own):
            s = i * halves + h
            rest_ref[2 * s : 2 * s + 1, :cut] = total[i : i + 1, h * cut : (h + 1) * cut]
            rest_ref[2 * s + 1 : 2 * s + 2, :cut] = target_rows[i : i + 1, h * cut : (h + 1) * cut]

    def summed(which):
        tiles_of = []
        for t in range(token_tiles):
            terms = [
                jnp.sum(take((which * 3 + term) * token_tiles + t), axis=0, keepdims=True)
                for term in range(3)
            ]
            tiles_of.append(terms[0] + terms[1] + terms[2])
        return tiles_of

    lane = lax.broadcasted_iota(jnp.int32, (own, LANES), 1)
    token = lax.broadcasted_iota(jnp.int32, (own, LANES), 0) + place_ref[0] * own
    score = jnp.zeros((own, 1), F32)
    for t, value in enumerate(summed(1)):
        score = score + jnp.sum(
            jnp.where(lane + t * LANES == token, jnp.broadcast_to(value, lane.shape), 0.0),
            axis=1,
            keepdims=True,
        )
    high, middle, low = three_terms(score)
    scores = jnp.where(lane == 0, high, jnp.where(lane == 1, middle, jnp.where(lane == 2, low, 0.0)))
    sums = [three_terms(value) for value in summed(0)]
    extra = [sums[t][term] for term in range(3) for t in range(token_tiles)]
    per_row = (len(extra) + 2) // 2
    for s in range(n_section):
        i = s // halves
        for n, value in enumerate(extra + [scores[i : i + 1]]):
            row, column = 2 * s + n // per_row, cut + n % per_row * LANES
            rest_ref[row : row + 1, column : column + LANES] = value
        for n in range(len(extra) + 1, 2 * per_row):
            row, column = 2 * s + n // per_row, cut + n % per_row * LANES
            rest_ref[row : row + 1, column : column + LANES] = jnp.zeros((1, LANES), F32)
    for s in range(n_section):
        out_ref[s] = rest_ref[2 * s : 2 * s + 2, :].astype(BF16)


def combine_body(in_ref, me_ref, mask_ref, out_ref, totals_ref, tokens_ref):
    n_section, _, piece_width = in_ref.shape
    cut = out_ref.shape[2]
    tokens = totals_ref.shape[1]
    own = out_ref.shape[0]
    halves = n_section // own
    total = in_ref[0].astype(F32)
    for s in range(1, n_section):
        total = total + in_ref[s].astype(F32)
    token_tiles = -(-tokens // LANES)
    per_row = (piece_width - cut) // LANES

    def tile_of(n):
        row, column = n // per_row, cut + n % per_row * LANES
        return total[row : row + 1, column : column + LANES]

    for t in range(token_tiles):
        tokens_ref[:, t * LANES : (t + 1) * LANES] = (
            tile_of(t) + tile_of(token_tiles + t) + tile_of(2 * token_tiles + t)
        )
    totals = tokens_ref[:, :tokens]
    totals_ref[...] = totals
    token = me_ref[1] * own + lax.div(me_ref[0], halves)
    here = lax.broadcasted_iota(jnp.int32, totals.shape, 1) == token
    whole = jnp.sum(jnp.where(here, totals, 0.0), axis=1, keepdims=True)
    weight = jnp.sum(jnp.where(here, mask_ref[...].astype(F32), 0.0), axis=1, keepdims=True)
    score = jnp.sum(tile_of(3 * token_tiles), axis=1, keepdims=True)
    bend = score * (1.0 / 30.0)
    at_target = weight * (jnp.exp(score) / whole - 1.0) * (1.0 - bend * bend)
    at_target = at_target.astype(BF16).astype(F32)
    grad = total[0:1, :cut] / whole + at_target * total[1:2, :cut]
    for s in range(out_ref.shape[0]):
        out_ref[s] = grad


def normed_rows(res_ref):
    x = res_ref[...].astype(F32)
    inverse = 1.0 / jnp.sqrt(jnp.mean(x * x, axis=1, keepdims=True) + 1e-06)
    return x * inverse, inverse


def gain_body(in_ref, core_ref, res_ref, out_ref):
    own, _, cut = in_ref.shape
    normed, _ = normed_rows(res_ref)
    half = jnp.where(core_ref[0] == 0, normed[:, :cut], normed[:, cut:])
    gain = jnp.sum(in_ref[:, 0, :] * half, axis=0, keepdims=True)
    for i in range(out_ref.shape[0]):
        out_ref[i] = gain


def close_body(in_ref, other_ref, core_ref, res_ref, gain_ref, grad_ref):
    mine, other = in_ref[:, 0, :], other_ref[:, 0, :]
    at_left = core_ref[0] == 0
    left, right = jnp.where(at_left, mine, other), jnp.where(at_left, other, mine)
    normed, inverse = normed_rows(res_ref)
    scaled = jnp.concatenate([left, right], axis=1) * gain_ref[...]
    along = jnp.mean(scaled * normed, axis=1, keepdims=True)
    grad_ref[...] = ((scaled - normed * along) * inverse).astype(BF16)


def compact_table_body(
    target_row_ref, totals_ref, mask_ref, res_ref, gain_ref, table_ref, slot_rows_ref, moved_ref,
    out_ref, hidden_ref, inverse_ref,
):
    vocab_rows, width = out_ref.shape
    capped = capped_scores(res_ref, gain_ref, table_ref, hidden_ref, inverse_ref)
    rows = lax.broadcasted_iota(jnp.int32, capped.shape, 0)
    hit = (target_row_ref[...] == rows).astype(F32)
    share = jnp.exp(capped) * (1.0 / totals_ref[...])
    bend = capped * (1.0 / 30.0)
    dlogits = (mask_ref[...].astype(F32) * (share - hit) * (1.0 - bend * bend)).astype(BF16)
    n_slots = moved_ref.shape[0]
    slot_iota = lax.broadcasted_iota(jnp.int32, (vocab_rows, n_slots), 0)
    onehot = (slot_rows_ref[1, :, :n_slots] == slot_iota).astype(F32).astype(BF16)
    scale = math.sqrt(width)
    tile = 2 * LANES
    for n in range(width // tile):
        columns = slice(n * tile, (n + 1) * tile)
        head = jnp.dot(dlogits, hidden_ref[:, columns], preferred_element_type=F32)
        inputs = jnp.dot(onehot, moved_ref[:, columns], preferred_element_type=F32)
        out_ref[:, columns] = (head + scale * inputs).astype(BF16)


def general(
    everyone, plan, residual, final_gain, table, targets, input_ids, loss_mask, embed_cotangent
):
    del plan
    own, width = residual.shape
    vocab_rows = table.shape[0]
    n_plane, n_section = lax.axis_size(PLANE), lax.axis_size(SECTION)
    tokens = own * n_plane
    cut = own * width // n_section
    n_lanes = width // LANES
    rider = -(-2 * n_lanes // own) * own
    product = 2 * tokens * vocab_rows * width
    shape = jax.ShapeDtypeStruct
    first = (lax.axis_index(EVERY) * vocab_rows).astype(jnp.int32).reshape(1)
    gain_row = final_gain.reshape(1, width)

    packed_width = width + rider // own * LANES
    norm_rooms = [pltpu.VMEM((tokens, width), BF16), pltpu.VMEM((tokens, LANES), F32)]
    rows_bytes = vocab_rows * width * 2

    wide = jnp.pad(embed_cotangent, ((0, 0), (0, 512)))
    all_cotangent = lax.all_gather(wide, PLANE, axis=0, tiled=True)

    sums = call(
        sums_body,
        shape((n_section, 1, tokens), F32),
        product,
        rows_bytes,
        everyone, gain_row, table,
        scratch=norm_rooms,
    )
    sums = call(
        spread_body, shape((n_plane, 1, tokens), F32), tokens, 4 * tokens, exchange(sums, SECTION)
    )
    given = (
        first, exchange(sums, PLANE), targets.reshape(1, tokens), loss_mask.reshape(1, tokens),
        everyone, gain_row, table,
    )
    packed = call(
        partial_body,
        shape((n_plane, own, packed_width), BF16),
        2 * product,
        rows_bytes,
        *given,
        in_specs=[SMEM] + [VMEM] * 6,
        scratch=norm_rooms + [pltpu.VMEM((rider, LANES), F32)],
    )
    arrived = exchange(packed, PLANE)
    split = call(
        split_body,
        shape((n_section, 1, cut + LANES), F32),
        tokens * width,
        tokens * width * 2,
        arrived,
        scratch=[pltpu.VMEM((rider, LANES), F32)],
    )
    reduced = call(
        spread_body,
        shape((n_section, 1, cut + LANES), F32),
        own * width,
        own * width * 8,
        exchange(split, SECTION),
    )
    grad_table = call(
        table_body,
        shape((vocab_rows, width), BF16),
        3 * product,
        2 * rows_bytes,
        *given, input_ids.reshape(1, tokens), all_cotangent,
        in_specs=[SMEM] + [VMEM] * 8,
        scratch=norm_rooms,
    )
    summed, grad_table = lax.optimization_barrier((exchange(reduced, SECTION), grad_table))
    grad_residual, grad_gain = call(
        finish_body,
        (shape((own, width), BF16), shape((n_lanes, LANES), F32)),
        own * width * 10,
        own * width * 8,
        summed, residual, gain_row,
    )
    return (grad_residual, grad_gain.reshape(width), grad_table)


def compact(
    everyone, plan, residual, final_gain, table, targets, input_ids, loss_mask, embed_cotangent
):
    del input_ids, embed_cotangent
    slot_rows, codes, slots, me = plan
    own, width = residual.shape
    vocab_rows = table.shape[0]
    n_plane, n_section = lax.axis_size(PLANE), lax.axis_size(SECTION)
    tokens = own * n_plane
    cut = own * width // n_section
    product = 2 * tokens * vocab_rows * width
    rows_bytes = vocab_rows * width * 2
    shape = jax.ShapeDtypeStruct
    _, token_tiles, scalar_tiles, slot_tiles = slot_layout(own, width, tokens)
    tiles = scalar_tiles + slot_tiles
    packed_width = width + tiles * LANES
    piece_width = cut + (3 * token_tiles + 2) // 2 * LANES
    norm_rooms = [pltpu.VMEM((tokens, width), BF16), pltpu.VMEM((tokens, LANES), F32)]
    gain_row = final_gain.reshape(1, width)
    mask = loss_mask.reshape(1, tokens)
    target_row = targets.reshape(1, tokens) - (me[0] * n_plane + me[1]) * vocab_rows

    packed = call(
        compact_body,
        shape((n_plane, own, packed_width), BF16),
        2 * product,
        rows_bytes,
        everyone, table, slots, gain_row, target_row, mask,
        in_specs=[ANY] * 3 + [VMEM] * 3,
        scratch=[
            pltpu.VMEM((tokens, width), BF16),
            pltpu.VMEM((vocab_rows, width), BF16),
            pltpu.VMEM((n_plane, own, slot_tiles * LANES), BF16),
        ] + norm_rooms + [
            pltpu.VMEM((1, token_tiles * LANES), F32),
            pltpu.VMEM((scalar_tiles * own, LANES), F32),
            pltpu.SemaphoreType.DMA((3,)),
        ],
    )
    pieces, moved = call(
        unpack_body,
        (
            shape((n_section, 2, piece_width), BF16),
            shape((SLOTS * n_plane, width), BF16),
        ),
        tokens * width,
        tokens * packed_width * 2,
        exchange(packed, PLANE), me[1:2], codes,
        in_specs=[VMEM, SMEM, VMEM],
        scratch=[
            pltpu.VMEM((n_plane * tiles * own, LANES), F32),
            pltpu.VMEM((SLOTS * n_plane, width), F32),
            pltpu.VMEM((2 * n_section, piece_width), F32),
        ],
    )
    half_token, totals = call(
        combine_body,
        (shape((own, 1, cut), F32), shape((1, tokens), F32)),
        own * width,
        own * width * 8,
        exchange(pieces, SECTION), me, mask,
        in_specs=[VMEM, SMEM, VMEM],
        scratch=[pltpu.VMEM((1, token_tiles * LANES), F32)],
    )
    grad_table = call(
        compact_table_body,
        shape((vocab_rows, width), BF16),
        3 * product,
        2 * rows_bytes,
        target_row, totals, mask, everyone, gain_row, table, slot_rows, moved,
        scratch=norm_rooms,
    )
    mine, grad_table = lax.optimization_barrier((exchange(half_token, "z"), grad_table))
    core = lax.axis_index("core").astype(jnp.int32).reshape(1)
    n_chips = lax.axis_size(CHIPS)
    other = lax.ppermute(mine, "core", [(0, 1), (1, 0)])
    gain_part = call(
        gain_body,
        shape((n_chips, 1, cut), F32),
        own * width * 4,
        own * width * 8,
        mine, core, residual,
        in_specs=[VMEM, SMEM, VMEM],
    )
    grad_residual = call(
        close_body,
        shape((own, width), BF16),
        own * width * 10,
        own * width * 8,
        mine, other, core, residual, gain_row,
        in_specs=[VMEM, VMEM, SMEM, VMEM, VMEM],
    )
    grad_gain = exchange(gain_part, CHIPS).reshape(n_chips // n_plane, n_plane, cut)
    return (grad_residual, jnp.sum(grad_gain, axis=1).reshape(width), grad_table)


def on_device(residual, final_gain, table, targets, input_ids, loss_mask, embed_cotangent):
    own, width = residual.shape
    n_plane = lax.axis_size(PLANE)
    shape = jax.ShapeDtypeStruct
    ids = jnp.stack([targets.reshape(n_plane, own).T, input_ids.reshape(n_plane, own).T])
    place = lax.axis_index(PLANE)
    me = jnp.stack([lax.axis_index(SECTION), place, table.shape[0], own]).astype(jnp.int32)
    lanes = -(-SLOTS * n_plane // LANES) * LANES
    everyone = exchange(jnp.broadcast_to(residual[None], (n_plane, own, width)), PLANE)
    everyone = everyone.reshape(n_plane * own, width)
    slot_rows, codes, pairs = call(
        plan_body,
        (
            shape((2, 1, lanes), jnp.int32),
            shape((2, own, lanes), jnp.int32),
            shape((2, own, n_plane), jnp.int32),
        ),
        1000,
        1000,
        ids, me,
        in_specs=[VMEM, SMEM],
    )
    pairs = pairs.reshape(-1)
    alike = (pairs[:, None] == pairs[None, :]) & (pairs[:, None] >= 0)
    fits = jnp.max(jnp.sum(alike.astype(jnp.int32), axis=1)) <= SLOTS
    slot_tiles = slot_layout(own, width, own * n_plane)[3]
    slots = call(
        slots_body,
        shape((n_plane, own, slot_tiles * LANES), BF16),
        1000,
        1000,
        table, slot_rows, codes, embed_cotangent,
        scratch=[pltpu.VMEM((n_plane * slot_tiles * own, LANES), F32)],
    )
    return lax.cond(
        fits,
        compact,
        general,
        everyone, (slot_rows, codes, slots, me), residual, final_gain, table, targets, input_ids, loss_mask,
        embed_cotangent,
    )


def solution(mesh):
    cores = 2
    devices = mesh.devices.reshape(-1, cores, *mesh.devices.shape[1:])
    fine = jax.sharding.Mesh(devices, EVERY)
    placed = (
        P(PLANE, None),
        P(),
        P(EVERY, None),
        P(),
        P(),
        P(),
        P(PLANE, None),
    )
    return jax.shard_map(
        on_device,
        mesh=fine,
        in_specs=placed,
        out_specs=(P(PLANE, None), P(), P(EVERY, None)),
        check_vma=False,
    )
```

```python
import functools
import math

import jax
import jax.numpy as jnp
from jax import lax
from jax.experimental import pallas as pl
from jax.experimental.pallas import tpu as pltpu
from jax.sharding import PartitionSpec as P

PLANE = ("tensor", "dp")
SECTION = ("z", "core")
CHIPS = ("core", "tensor", "dp")
EVERY = ("z", "core", "tensor", "dp")
LANES = 128
SLOTS = 3
VMEM_LIMIT = 24 * 1024 * 1024
F32 = jnp.float32
BF16 = jnp.bfloat16
VMEM = pl.BlockSpec(memory_space=pltpu.VMEM)
ANY = pl.BlockSpec(memory_space=pl.ANY)
SMEM = pl.BlockSpec(memory_space=pltpu.SMEM)


def exchange(pieces, axes):
    return lax.all_to_all(pieces, axes, 0, 0, tiled=True)


def call(body, outs, flops, moved, *operands, in_specs=None, out_specs=None, scratch=()):
    several = isinstance(outs, tuple)
    return pl.pallas_call(
        body,
        out_shape=outs,
        in_specs=in_specs or [VMEM] * len(operands),
        out_specs=out_specs or ((VMEM,) * len(outs) if several else VMEM),
        scratch_shapes=list(scratch),
        compiler_params=pltpu.CompilerParams(vmem_limit_bytes=VMEM_LIMIT),
        cost_estimate=pl.CostEstimate(flops=flops, bytes_accessed=moved, transcendentals=0),
    )(*operands)


def norm_rows(res_ref, gain_ref, hidden_ref, inverse_ref):
    tokens = res_ref.shape[0]
    step = 16

    def norm(i, carry):
        rows = pl.ds(pl.multiple_of(i * step, step), step)
        x = res_ref[rows, :].astype(F32)
        inverse = 1.0 / jnp.sqrt(jnp.mean(x * x, axis=1, keepdims=True) + 1e-06)
        inverse_ref[rows, :] = jnp.broadcast_to(inverse, (step, LANES))
        hidden_ref[rows, :] = (x * inverse * gain_ref[...]).astype(BF16)
        return carry

    lax.fori_loop(0, tokens // step, norm, 0, unroll=16)


def scores_of(table_ref, hidden_ref):
    vocab_rows, block = table_ref.shape[0], 256
    scores = [
        lax.dot_general(
            table_ref[start : min(start + block, vocab_rows), :],
            hidden_ref[...],
            (((1,), (1,)), ((), ())),
            preferred_element_type=F32,
        )
        for start in range(0, vocab_rows, block)
    ]
    scores = jnp.concatenate(scores, axis=0)
    return 30.0 * jnp.tanh(scores * (1.0 / 30.0))


def capped_scores(res_ref, gain_ref, table_ref, hidden_ref, inverse_ref):
    norm_rows(res_ref, gain_ref, hidden_ref, inverse_ref)
    return scores_of(table_ref, hidden_ref)


def logit_grads(capped, first_ref, arrived_ref, targets_ref, mask_ref):
    totals = arrived_ref[0]
    for i in range(1, arrived_ref.shape[0]):
        totals = totals + arrived_ref[i]
    rows = lax.broadcasted_iota(jnp.int32, capped.shape, 0)
    hit = (targets_ref[...] - first_ref[0] == rows).astype(F32)
    share = jnp.exp(capped) * (1.0 / totals)
    bend = capped * (1.0 / 30.0)
    return (mask_ref[...].astype(F32) * (share - hit) * (1.0 - bend * bend)).astype(BF16)


def sums_body(vocab_rows, res_ref, gain_ref, table_ref, sums_ref, hidden_ref, inverse_ref):
    capped = capped_scores(res_ref, gain_ref, table_ref, hidden_ref, inverse_ref)
    rows = lax.broadcasted_iota(jnp.int32, capped.shape, 0)
    sums = jnp.sum(jnp.where(rows < vocab_rows, jnp.exp(capped), 0.0), axis=0, keepdims=True)
    for i in range(sums_ref.shape[0]):
        sums_ref[i] = sums


def spread_body(in_ref, out_ref):
    total = in_ref[0]
    for i in range(1, in_ref.shape[0]):
        total = total + in_ref[i]
    for i in range(out_ref.shape[0]):
        out_ref[i] = total


def partial_body(
    first_ref, arrived_ref, targets_ref, mask_ref, res_ref, gain_ref, table_ref,
    packed_ref, hidden_ref, inverse_ref, rider_ref,
):
    n_plane, own, packed_width = packed_ref.shape
    width = res_ref.shape[1]
    capped = capped_scores(res_ref, gain_ref, table_ref, hidden_ref, inverse_ref)
    dlogits = logit_grads(capped, first_ref, arrived_ref, targets_ref, mask_ref)
    rider_ref[...] = jnp.zeros_like(rider_ref)
    tile = 2 * LANES
    n_lanes = width // LANES
    inverse = jnp.concatenate([inverse_ref[...]] * 2, axis=1)
    for n in range(width // tile):
        columns = slice(n * tile, (n + 1) * tile)
        part = lax.dot_general(
            dlogits, table_ref[:, columns], (((0,), (0,)), ((), ())), preferred_element_type=F32
        )
        packed_ref[:, :, columns] = part.astype(BF16).reshape(n_plane, own, tile)
        normed = res_ref[:, columns].astype(F32) * inverse
        gain = jnp.sum(part * normed, axis=0, keepdims=True)
        high = gain.astype(BF16).astype(F32)
        low = gain - high
        for k in range(2):
            piece = slice(k * LANES, (k + 1) * LANES)
            rider_ref[2 * n + k : 2 * n + k + 1, :] = high[:, piece]
            rider_ref[n_lanes + 2 * n + k : n_lanes + 2 * n + k + 1, :] = low[:, piece]
    for j in range(rider_ref.shape[0] // own):
        block = rider_ref[j * own : (j + 1) * own, :].astype(BF16)
        for i in range(n_plane):
            packed_ref[i, :, width + j * LANES : width + (j + 1) * LANES] = block


def split_body(in_ref, out_ref, gain_ref):
    n_plane, own, packed_width = in_ref.shape
    n_section = out_ref.shape[0]
    cut = out_ref.shape[2] - LANES
    halves = n_section // own
    width = halves * cut
    n_lanes = width // LANES
    total = in_ref[0].astype(F32)
    for i in range(1, n_plane):
        total = total + in_ref[i].astype(F32)
    for h in range(halves):
        out_ref[h * own : (h + 1) * own, 0, :cut] = total[:, h * cut : (h + 1) * cut]
    for j in range((packed_width - width) // LANES):
        gain_ref[j * own : (j + 1) * own, :] = total[:, width + j * LANES : width + (j + 1) * LANES]
    rows = gain_ref[:n_lanes, :] + gain_ref[n_lanes : 2 * n_lanes, :]
    out_ref[:n_lanes, 0, cut:] = rows
    out_ref[n_lanes:, 0, cut:] = jnp.zeros((n_section - n_lanes, LANES), F32)


def finish_body(in_ref, res_ref, gain_ref, grad_ref, grad_gain_ref):
    n_section = in_ref.shape[0]
    own, width = res_ref.shape
    cut = in_ref.shape[2] - LANES
    halves = n_section // own
    x = res_ref[...].astype(F32)
    inverse = 1.0 / jnp.sqrt(jnp.mean(x * x, axis=1, keepdims=True) + 1e-06)
    normed = x * inverse
    grad_hidden = jnp.concatenate(
        [in_ref[h * own : (h + 1) * own, 0, :cut] for h in range(halves)], axis=1
    )
    scaled = grad_hidden * gain_ref[...]
    along = jnp.mean(scaled * normed, axis=1, keepdims=True)
    grad_ref[...] = ((scaled - normed * along) * inverse).astype(BF16)
    grad_gain_ref[...] = in_ref[: width // LANES, 0, cut:]


def table_body(
    first_ref, arrived_ref, targets_ref, mask_ref, res_ref, gain_ref, table_ref, ids_ref,
    cotangent_ref, out_ref, hidden_ref, inverse_ref,
):
    vocab_rows, width = out_ref.shape
    capped = capped_scores(res_ref, gain_ref, table_ref, hidden_ref, inverse_ref)
    dlogits = logit_grads(capped, first_ref, arrived_ref, targets_ref, mask_ref)
    rows = lax.broadcasted_iota(jnp.int32, capped.shape, 0)
    onehot = (ids_ref[...] - first_ref[0] == rows).astype(F32).astype(BF16)
    scale = math.sqrt(width)
    tile = 2 * LANES
    for n in range(width // tile):
        columns = slice(n * tile, (n + 1) * tile)
        head = jnp.dot(dlogits, hidden_ref[:, columns], preferred_element_type=F32)
        inputs = jnp.dot(onehot, cotangent_ref[:, columns], preferred_element_type=F32)
        out_ref[:, columns] = (head + scale * inputs)[:vocab_rows].astype(BF16)


def plan_body(ids_ref, me_ref, rows_ref, codes_ref, pairs_ref):
    _, own, groups = ids_ref.shape
    section, place, vocab_rows = me_ref[0], me_ref[1], me_ref[2]
    device = section * groups + place
    token = lax.broadcasted_iota(jnp.int32, (own, groups), 0)
    group = lax.broadcasted_iota(jnp.int32, (own, groups), 1)

    def column(x):
        return jnp.sum(jnp.where(group == place, x, 0), axis=1, keepdims=True)

    ahead_sent = ahead_here = jnp.zeros((1, groups), jnp.int32)
    for which in range(2):
        ids = ids_ref[which]
        owner = lax.div(ids, vocab_rows)
        again = jnp.zeros(ids.shape, jnp.int32)
        for j in range(own):
            again = again + jnp.where((ids == ids[j : j + 1]) & (token > j), 1, 0)
        first = jnp.where(again == 0, 1, 0)
        slot = jnp.zeros(ids.shape, jnp.int32)
        for j in range(own):
            under = (owner == owner[j : j + 1]) & (ids[j : j + 1] < ids) & (first[j : j + 1] == 1)
            slot = slot + jnp.where(under, 1, 0)
        near = column(owner) - section * groups
        inside = (near >= 0) & (near < groups)
        mine = (owner == device) & (first == 1)
        if which == 0:
            offset = jnp.zeros((own, 1), jnp.int32)
            pair = owner * groups + group
        else:
            offset = jnp.sum(jnp.where(group == near, ahead_sent, 0), axis=1, keepdims=True)
            slot_here = slot + ahead_here
            over = lax.div(owner, groups) * groups
            pair = (over + group) * groups + owner - over
        pairs_ref[which] = jnp.where(first == 1, pair, -1)
        code = jnp.where(inside, (column(slot) + offset) * groups + near, -1)
        codes_ref[which] = jnp.broadcast_to(code, codes_ref.shape[1:])
        rows_ref[which] = jnp.full(rows_ref.shape[1:], -1, jnp.int32)
        for k in range(SLOTS):
            taken = mine & ((slot if which == 0 else slot_here) == k)
            local = jnp.where(taken, ids - device * vocab_rows + 1, 0)
            rows_ref[which, :, k * groups : (k + 1) * groups] = (
                jnp.sum(local, axis=0, keepdims=True) - 1
            )
        if which == 0:
            ahead_sent = jnp.sum(jnp.where(mine, 1, 0), axis=0, keepdims=True)
            come = (group == near) & (column(first) == 1)
            ahead_here = jnp.sum(jnp.where(come, 1, 0), axis=0, keepdims=True)


def three_terms(x):
    high = x.astype(BF16).astype(F32)
    middle = (x - high).astype(BF16).astype(F32)
    return high, middle, x - high - middle


def slot_layout(own, width, tokens):
    n_lanes = width // LANES
    token_tiles = -(-tokens // LANES)
    scalar_tiles = -(-6 * token_tiles // own)
    slot_tiles = -(-SLOTS * n_lanes // own)
    return n_lanes, token_tiles, scalar_tiles, slot_tiles


def slots_body(
    table_ref, slot_rows_ref, codes_ref, cotangent_ref, out_ref, tail_ref, room_ref
):
    n_plane, own, _ = out_ref.shape
    vocab_rows, width = table_ref.shape
    n_lanes, _, _, tiles = slot_layout(own, width, own * n_plane)
    stride = tiles * own

    def put(at, value):
        room_ref[pl.ds(at, n_plane, stride=stride), :] = value

    for at in range(SLOTS * n_lanes, stride):
        put(at, jnp.zeros((n_plane, LANES), F32))
    n_slots = SLOTS * n_plane
    slot_iota = lax.broadcasted_iota(jnp.int32, (vocab_rows, n_slots), 0)
    pick = (slot_rows_ref[0, :, :n_slots] == slot_iota).astype(F32).astype(BF16)
    last = tail_ref.shape[0]
    last_start = (vocab_rows - 1) // last * last
    last_rows = lax.broadcasted_iota(jnp.int32, (vocab_rows, last), 0) - last_start
    pick_last = last_rows == lax.broadcasted_iota(jnp.int32, (vocab_rows, last), 1)
    pick_last = pick_last.astype(F32).astype(BF16)
    own_iota = lax.broadcasted_iota(jnp.int32, (own, n_slots), 1)
    give = (codes_ref[1, :, :n_slots] == own_iota).astype(F32).astype(BF16)
    dims = (((0,), (0,)), ((), ()))
    tile = 2 * LANES
    for n in range(width // tile):
        columns = slice(n * tile, (n + 1) * tile)
        rows = table_ref[:, columns]
        tail_ref[:, columns] = lax.dot_general(
            pick_last, rows, dims, preferred_element_type=F32
        ).astype(BF16)
        moved = lax.dot_general(pick, rows, dims, preferred_element_type=F32)
        moved = moved + lax.dot_general(
            give, cotangent_ref[:, columns], dims, preferred_element_type=F32
        )
        for k in range(SLOTS):
            block = moved[k * n_plane : (k + 1) * n_plane]
            for half in range(2):
                put(k * n_lanes + 2 * n + half, block[:, half * LANES : (half + 1) * LANES])
    for p in range(n_plane):
        for t in range(tiles):
            start = p * stride + t * own
            out_ref[p, :, t * LANES : (t + 1) * LANES] = (
                room_ref[start : start + own, :].astype(BF16)
            )


def whole_rows(table_hbm, table_ref, sem):
    rows = table_ref.shape[0] - 16
    return pltpu.make_async_copy(table_hbm.at[:rows, :], table_ref.at[:rows, :], sem)


def compact_body(
    vocab_rows, me_ref, res_hbm, table_hbm, slots_hbm, tail_ref, gain_ref, targets_ref, mask_ref,
    packed_ref, res_ref, table_ref, slots_ref, hidden_ref, inverse_ref, tokens_ref, room_ref, sems,
):
    copies = [
        pltpu.make_async_copy(res_hbm, res_ref, sems.at[0]),
        whole_rows(table_hbm, table_ref, sems.at[1]),
        pltpu.make_async_copy(slots_hbm, slots_ref, sems.at[2]),
    ]
    for copy in copies:
        copy.start()
    n_plane, own, packed_width = packed_ref.shape
    tokens, width = res_ref.shape
    n_lanes, token_tiles, scalar_tiles, _ = slot_layout(own, width, tokens)
    copies[0].wait()
    norm_rows(res_ref, gain_ref, hidden_ref, inverse_ref)
    copies[1].wait()
    table_ref[table_ref.shape[0] - tail_ref.shape[0] :, :] = tail_ref[...]
    capped = scores_of(table_ref, hidden_ref)
    rows = lax.broadcasted_iota(jnp.int32, capped.shape, 0)
    device = me_ref[0] * n_plane + me_ref[1]
    hit = targets_ref[...] - device * vocab_rows == rows
    expterm = jnp.where(rows < vocab_rows, jnp.exp(capped), 0.0)
    bend = capped * (1.0 / 30.0)
    weight = mask_ref[...].astype(F32) * (1.0 - bend * bend)
    unscaled = jnp.where(hit, 0.0, weight * expterm).astype(BF16)
    pieces = [
        jnp.sum(expterm, axis=0, keepdims=True),
        jnp.sum(jnp.where(hit, capped, 0.0), axis=0, keepdims=True),
    ]
    tokens_ref[...] = jnp.zeros_like(tokens_ref)
    room_ref[...] = jnp.zeros_like(room_ref)
    for which in range(2):
        for term, value in enumerate(three_terms(pieces[which])):
            tokens_ref[:, :tokens] = value
            for t in range(token_tiles):
                at = (which * 3 + term) * token_tiles + t
                room_ref[at : at + 1, :] = tokens_ref[:, t * LANES : (t + 1) * LANES]
    for t in range(scalar_tiles):
        block = room_ref[t * own : (t + 1) * own, :].astype(BF16)
        for p in range(n_plane):
            packed_ref[p, :, width + t * LANES : width + (t + 1) * LANES] = block
    tile = 2 * LANES
    for n in range(width // tile):
        columns = slice(n * tile, (n + 1) * tile)
        part = lax.dot_general(
            unscaled, table_ref[:, columns], (((0,), (0,)), ((), ())), preferred_element_type=F32
        )
        packed_ref[:, :, columns] = part.astype(BF16).reshape(n_plane, own, tile)
    copies[2].wait()
    packed_ref[:, :, width + scalar_tiles * LANES :] = slots_ref[...]


def unpack_body(
    in_ref, place_ref, codes_ref, out_ref, rows_out_ref, room_ref, moved_ref, rest_ref
):
    n_plane, own, packed_width = in_ref.shape
    tokens = n_plane * own
    n_section = out_ref.shape[0]
    halves = n_section // own
    width = rows_out_ref.shape[1]
    cut = width // halves
    n_lanes, token_tiles, scalar_tiles, slot_tiles = slot_layout(own, width, tokens)
    tiles = scalar_tiles + slot_tiles
    stride = tiles * own
    total = in_ref[0, :, :width].astype(F32)
    for p in range(1, n_plane):
        total = total + in_ref[p, :, :width].astype(F32)
    for p in range(n_plane):
        for t in range(tiles):
            start = p * stride + t * own
            room_ref[start : start + own, :] = in_ref[
                p, :, width + t * LANES : width + (t + 1) * LANES
            ].astype(F32)

    def take(at):
        return room_ref[pl.ds(at, n_plane, stride=stride), :]

    for k in range(SLOTS):
        for j in range(n_lanes):
            moved_ref[k * n_plane : (k + 1) * n_plane, j * LANES : (j + 1) * LANES] = take(
                scalar_tiles * own + k * n_lanes + j
            )
    moved = moved_ref[...].astype(BF16)
    rows_out_ref[...] = moved
    n_slots = SLOTS * n_plane
    own_iota = lax.broadcasted_iota(jnp.int32, (own, n_slots), 1)
    choose = (codes_ref[0, :, :n_slots] == own_iota).astype(F32).astype(BF16)
    target_rows = jnp.dot(choose, moved, preferred_element_type=F32)
    for h in range(halves):
        for i in range(own):
            s = i * halves + h
            rest_ref[2 * s : 2 * s + 1, :cut] = total[i : i + 1, h * cut : (h + 1) * cut]
            rest_ref[2 * s + 1 : 2 * s + 2, :cut] = target_rows[i : i + 1, h * cut : (h + 1) * cut]

    def summed(which):
        tiles_of = []
        for t in range(token_tiles):
            terms = [
                jnp.sum(take((which * 3 + term) * token_tiles + t), axis=0, keepdims=True)
                for term in range(3)
            ]
            tiles_of.append(terms[0] + terms[1] + terms[2])
        return tiles_of

    lane = lax.broadcasted_iota(jnp.int32, (own, LANES), 1)
    token = lax.broadcasted_iota(jnp.int32, (own, LANES), 0) + place_ref[0] * own
    score = jnp.zeros((own, 1), F32)
    for t, value in enumerate(summed(1)):
        score = score + jnp.sum(
            jnp.where(lane + t * LANES == token, jnp.broadcast_to(value, lane.shape), 0.0),
            axis=1,
            keepdims=True,
        )
    high, middle, low = three_terms(score)
    scores = jnp.where(lane == 0, high, jnp.where(lane == 1, middle, jnp.where(lane == 2, low, 0.0)))
    sums = [three_terms(value) for value in summed(0)]
    extra = [sums[t][term] for term in range(3) for t in range(token_tiles)]
    per_row = (len(extra) + 2) // 2
    for s in range(n_section):
        i = s // halves
        for n, value in enumerate(extra + [scores[i : i + 1]]):
            row, column = 2 * s + n // per_row, cut + n % per_row * LANES
            rest_ref[row : row + 1, column : column + LANES] = value
        for n in range(len(extra) + 1, 2 * per_row):
            row, column = 2 * s + n // per_row, cut + n % per_row * LANES
            rest_ref[row : row + 1, column : column + LANES] = jnp.zeros((1, LANES), F32)
    for s in range(n_section):
        out_ref[s] = rest_ref[2 * s : 2 * s + 2, :].astype(BF16)


def combine_body(in_ref, me_ref, mask_ref, out_ref, totals_ref, tokens_ref):
    n_section, _, piece_width = in_ref.shape
    cut = out_ref.shape[2]
    tokens = totals_ref.shape[1]
    own = out_ref.shape[0]
    halves = n_section // own
    total = in_ref[0].astype(F32)
    for s in range(1, n_section):
        total = total + in_ref[s].astype(F32)
    token_tiles = -(-tokens // LANES)
    per_row = (piece_width - cut) // LANES

    def tile_of(n):
        row, column = n // per_row, cut + n % per_row * LANES
        return total[row : row + 1, column : column + LANES]

    for t in range(token_tiles):
        tokens_ref[:, t * LANES : (t + 1) * LANES] = (
            tile_of(t) + tile_of(token_tiles + t) + tile_of(2 * token_tiles + t)
        )
    totals = tokens_ref[:, :tokens]
    totals_ref[...] = totals
    token = me_ref[1] * own + lax.div(me_ref[0], halves)
    here = lax.broadcasted_iota(jnp.int32, totals.shape, 1) == token
    whole = jnp.sum(jnp.where(here, totals, 0.0), axis=1, keepdims=True)
    weight = jnp.sum(jnp.where(here, mask_ref[...].astype(F32), 0.0), axis=1, keepdims=True)
    score = jnp.sum(tile_of(3 * token_tiles), axis=1, keepdims=True)
    bend = score * (1.0 / 30.0)
    at_target = weight * (jnp.exp(score) / whole - 1.0) * (1.0 - bend * bend)
    at_target = at_target.astype(BF16).astype(F32)
    grad = total[0:1, :cut] / whole + at_target * total[1:2, :cut]
    for s in range(out_ref.shape[0]):
        out_ref[s] = grad


def normed_rows(res_ref):
    x = res_ref[...].astype(F32)
    inverse = 1.0 / jnp.sqrt(jnp.mean(x * x, axis=1, keepdims=True) + 1e-06)
    return x * inverse, inverse


def gain_body(in_ref, core_ref, res_ref, out_ref):
    own, _, cut = in_ref.shape
    normed, _ = normed_rows(res_ref)
    half = jnp.where(core_ref[0] == 0, normed[:, :cut], normed[:, cut:])
    gain = jnp.sum(in_ref[:, 0, :] * half, axis=0, keepdims=True)
    for i in range(out_ref.shape[0]):
        out_ref[i] = gain


def close_body(in_ref, other_ref, core_ref, res_ref, gain_ref, grad_ref):
    mine, other = in_ref[:, 0, :], other_ref[:, 0, :]
    at_left = core_ref[0] == 0
    left, right = jnp.where(at_left, mine, other), jnp.where(at_left, other, mine)
    normed, inverse = normed_rows(res_ref)
    scaled = jnp.concatenate([left, right], axis=1) * gain_ref[...]
    along = jnp.mean(scaled * normed, axis=1, keepdims=True)
    grad_ref[...] = ((scaled - normed * along) * inverse).astype(BF16)


def compact_table_body(
    me_ref, table_hbm, tail_ref, targets_ref, totals_ref, mask_ref, res_ref, gain_ref, slot_rows_ref,
    moved_ref, out_ref, table_ref, hidden_ref, inverse_ref, sem,
):
    vocab_rows, width = out_ref.shape
    copy = whole_rows(table_hbm, table_ref, sem)
    copy.start()
    norm_rows(res_ref, gain_ref, hidden_ref, inverse_ref)
    copy.wait()
    table_ref[table_ref.shape[0] - tail_ref.shape[0] :, :] = tail_ref[...]
    capped = scores_of(table_ref, hidden_ref)
    rows = lax.broadcasted_iota(jnp.int32, capped.shape, 0)
    device = me_ref[0] * (moved_ref.shape[0] // SLOTS) + me_ref[1]
    hit = (targets_ref[...] - device * vocab_rows == rows).astype(F32)
    share = jnp.exp(capped) * (1.0 / totals_ref[...])
    bend = capped * (1.0 / 30.0)
    dlogits = (mask_ref[...].astype(F32) * (share - hit) * (1.0 - bend * bend)).astype(BF16)
    n_slots = moved_ref.shape[0]
    slot_iota = lax.broadcasted_iota(jnp.int32, (capped.shape[0], n_slots), 0)
    onehot = (slot_rows_ref[1, :, :n_slots] == slot_iota).astype(F32).astype(BF16)
    scale = math.sqrt(width)
    tile = 2 * LANES
    for n in range(width // tile):
        columns = slice(n * tile, (n + 1) * tile)
        head = jnp.dot(dlogits, hidden_ref[:, columns], preferred_element_type=F32)
        inputs = jnp.dot(onehot, moved_ref[:, columns], preferred_element_type=F32)
        out_ref[:, columns] = (head + scale * inputs)[:vocab_rows].astype(BF16)


def general(
    everyone, plan, residual, final_gain, table, targets, input_ids, loss_mask, embed_cotangent
):
    del plan
    padded = jnp.pad(table, ((0, -table.shape[0] % 16), (0, 0)))
    own, width = residual.shape
    vocab_rows = table.shape[0]
    n_plane, n_section = lax.axis_size(PLANE), lax.axis_size(SECTION)
    tokens = own * n_plane
    cut = own * width // n_section
    n_lanes = width // LANES
    rider = -(-2 * n_lanes // own) * own
    product = 2 * tokens * vocab_rows * width
    shape = jax.ShapeDtypeStruct
    first = (lax.axis_index(EVERY) * vocab_rows).astype(jnp.int32).reshape(1)
    gain_row = final_gain.reshape(1, width)

    packed_width = width + rider // own * LANES
    norm_rooms = [pltpu.VMEM((tokens, width), BF16), pltpu.VMEM((tokens, LANES), F32)]
    rows_bytes = vocab_rows * width * 2

    wide = jnp.pad(embed_cotangent, ((0, 0), (0, 512)))
    all_cotangent = lax.all_gather(wide, PLANE, axis=0, tiled=True)

    sums = call(
        functools.partial(sums_body, vocab_rows),
        shape((n_section, 1, tokens), F32),
        product,
        rows_bytes,
        everyone, gain_row, padded,
        scratch=norm_rooms,
    )
    sums = call(
        spread_body, shape((n_plane, 1, tokens), F32), tokens, 4 * tokens, exchange(sums, SECTION)
    )
    given = (
        first, exchange(sums, PLANE), targets.reshape(1, tokens), loss_mask.reshape(1, tokens),
        everyone, gain_row, padded,
    )
    packed = call(
        partial_body,
        shape((n_plane, own, packed_width), BF16),
        2 * product,
        rows_bytes,
        *given,
        in_specs=[SMEM] + [VMEM] * 6,
        scratch=norm_rooms + [pltpu.VMEM((rider, LANES), F32)],
    )
    arrived = exchange(packed, PLANE)
    split = call(
        split_body,
        shape((n_section, 1, cut + LANES), F32),
        tokens * width,
        tokens * width * 2,
        arrived,
        scratch=[pltpu.VMEM((rider, LANES), F32)],
    )
    reduced = call(
        spread_body,
        shape((n_section, 1, cut + LANES), F32),
        own * width,
        own * width * 8,
        exchange(split, SECTION),
    )
    grad_table = call(
        table_body,
        shape((vocab_rows, width), BF16),
        3 * product,
        2 * rows_bytes,
        *given, input_ids.reshape(1, tokens), all_cotangent,
        in_specs=[SMEM] + [VMEM] * 8,
        scratch=norm_rooms,
    )
    summed, grad_table = lax.optimization_barrier((exchange(reduced, SECTION), grad_table))
    grad_residual, grad_gain = call(
        finish_body,
        (shape((own, width), BF16), shape((n_lanes, LANES), F32)),
        own * width * 10,
        own * width * 8,
        summed, residual, gain_row,
    )
    return (grad_residual, grad_gain.reshape(width), grad_table)


def compact(
    everyone, plan, residual, final_gain, table, targets, input_ids, loss_mask, embed_cotangent
):
    del input_ids, embed_cotangent
    slot_rows, codes, slots, me, tail = plan
    own, width = residual.shape
    vocab_rows = table.shape[0]
    n_plane, n_section = lax.axis_size(PLANE), lax.axis_size(SECTION)
    tokens = own * n_plane
    cut = own * width // n_section
    product = 2 * tokens * vocab_rows * width
    rows_bytes = vocab_rows * width * 2
    shape = jax.ShapeDtypeStruct
    _, token_tiles, scalar_tiles, slot_tiles = slot_layout(own, width, tokens)
    tiles = scalar_tiles + slot_tiles
    packed_width = width + tiles * LANES
    piece_width = cut + (3 * token_tiles + 2) // 2 * LANES
    norm_rooms = [pltpu.VMEM((tokens, width), BF16), pltpu.VMEM((tokens, LANES), F32)]
    gain_row = final_gain.reshape(1, width)
    mask = loss_mask.reshape(1, tokens)
    targets = targets.reshape(1, tokens)

    table_room = pltpu.VMEM((-(-vocab_rows // 16) * 16, width), BF16)
    packed = call(
        functools.partial(compact_body, vocab_rows),
        shape((n_plane, own, packed_width), BF16),
        2 * product,
        rows_bytes,
        me, everyone, table, slots, tail, gain_row, targets, mask,
        in_specs=[SMEM] + [ANY] * 3 + [VMEM] * 4,
        scratch=[
            pltpu.VMEM((tokens, width), BF16),
            table_room,
            pltpu.VMEM((n_plane, own, slot_tiles * LANES), BF16),
        ] + norm_rooms + [
            pltpu.VMEM((1, token_tiles * LANES), F32),
            pltpu.VMEM((scalar_tiles * own, LANES), F32),
            pltpu.SemaphoreType.DMA((3,)),
        ],
    )
    pieces, moved = call(
        unpack_body,
        (
            shape((n_section, 2, piece_width), BF16),
            shape((SLOTS * n_plane, width), BF16),
        ),
        tokens * width,
        tokens * packed_width * 2,
        exchange(packed, PLANE), me[1:2], codes,
        in_specs=[VMEM, SMEM, VMEM],
        scratch=[
            pltpu.VMEM((n_plane * tiles * own, LANES), F32),
            pltpu.VMEM((SLOTS * n_plane, width), F32),
            pltpu.VMEM((2 * n_section, piece_width), F32),
        ],
    )
    half_token, totals = call(
        combine_body,
        (shape((own, 1, cut), F32), shape((1, tokens), F32)),
        own * width,
        own * width * 8,
        exchange(pieces, SECTION), me, mask,
        in_specs=[VMEM, SMEM, VMEM],
        scratch=[pltpu.VMEM((1, token_tiles * LANES), F32)],
    )
    grad_table = call(
        compact_table_body,
        shape((vocab_rows, width), BF16),
        3 * product,
        2 * rows_bytes,
        me, table, tail, targets, totals, mask, everyone, gain_row, slot_rows, moved,
        in_specs=[SMEM, ANY] + [VMEM] * 8,
        scratch=[table_room] + norm_rooms + [pltpu.SemaphoreType.DMA],
    )
    mine, grad_table = lax.optimization_barrier((exchange(half_token, "z"), grad_table))
    core = lax.axis_index("core").astype(jnp.int32).reshape(1)
    n_chips = lax.axis_size(CHIPS)
    other = lax.ppermute(mine, "core", [(0, 1), (1, 0)])
    gain_part = call(
        gain_body,
        shape((n_chips, 1, cut), F32),
        own * width * 4,
        own * width * 8,
        mine, core, residual,
        in_specs=[VMEM, SMEM, VMEM],
    )
    grad_residual = call(
        close_body,
        shape((own, width), BF16),
        own * width * 10,
        own * width * 8,
        mine, other, core, residual, gain_row,
        in_specs=[VMEM, VMEM, SMEM, VMEM, VMEM],
    )
    grad_gain = exchange(gain_part, CHIPS).reshape(n_chips // n_plane, n_plane, cut)
    return (grad_residual, jnp.sum(grad_gain, axis=1).reshape(width), grad_table)


def on_device(residual, final_gain, table, targets, input_ids, loss_mask, embed_cotangent):
    own, width = residual.shape
    n_plane = lax.axis_size(PLANE)
    shape = jax.ShapeDtypeStruct
    ids = jnp.stack([targets.reshape(n_plane, own).T, input_ids.reshape(n_plane, own).T])
    place = lax.axis_index(PLANE)
    me = jnp.stack([lax.axis_index(SECTION), place, table.shape[0], own]).astype(jnp.int32)
    lanes = -(-SLOTS * n_plane // LANES) * LANES
    everyone = exchange(jnp.broadcast_to(residual[None], (n_plane, own, width)), PLANE)
    everyone = everyone.reshape(n_plane * own, width)
    slot_rows, codes, pairs = call(
        plan_body,
        (
            shape((2, 1, lanes), jnp.int32),
            shape((2, own, lanes), jnp.int32),
            shape((2, own, n_plane), jnp.int32),
        ),
        1000,
        1000,
        ids, me,
        in_specs=[VMEM, SMEM],
    )
    pairs = pairs.reshape(-1)
    alike = (pairs[:, None] == pairs[None, :]) & (pairs[:, None] >= 0)
    fits = jnp.max(jnp.sum(alike.astype(jnp.int32), axis=1)) <= SLOTS
    slot_tiles = slot_layout(own, width, own * n_plane)[3]
    slots, tail = call(
        slots_body,
        (shape((n_plane, own, slot_tiles * LANES), BF16), shape((16, width), BF16)),
        1000,
        1000,
        table, slot_rows, codes, embed_cotangent,
        scratch=[pltpu.VMEM((n_plane * slot_tiles * own, LANES), F32)],
    )
    return lax.cond(
        fits,
        compact,
        general,
        everyone, (slot_rows, codes, slots, me, tail), residual, final_gain, table, targets, input_ids, loss_mask,
        embed_cotangent,
    )


def solution(mesh):
    cores = 2
    devices = mesh.devices.reshape(-1, cores, *mesh.devices.shape[1:])
    fine = jax.sharding.Mesh(devices, EVERY)
    placed = (
        P(PLANE, None),
        P(),
        P(EVERY, None),
        P(),
        P(),
        P(),
        P(PLANE, None),
    )
    return jax.shard_map(
        on_device,
        mesh=fine,
        in_specs=placed,
        out_specs=(P(PLANE, None), P(), P(EVERY, None)),
        check_vma=False,
    )
```

```python
import functools
import math

import jax
import jax.numpy as jnp
from jax import lax
from jax.experimental import pallas as pl
from jax.experimental.pallas import tpu as pltpu
from jax.sharding import PartitionSpec as P

PLANE = ("tensor", "dp")
SECTION = ("z", "core")
CHIPS = ("core", "tensor", "dp")
EVERY = ("z", "core", "tensor", "dp")
LANES = 128
SLOTS = 3
VMEM_LIMIT = 24 * 1024 * 1024
F32 = jnp.float32
BF16 = jnp.bfloat16
VMEM = pl.BlockSpec(memory_space=pltpu.VMEM)
ANY = pl.BlockSpec(memory_space=pl.ANY)
SMEM = pl.BlockSpec(memory_space=pltpu.SMEM)


def exchange(pieces, axes):
    return lax.all_to_all(pieces, axes, 0, 0, tiled=True)


def call(body, outs, flops, moved, *operands, in_specs=None, out_specs=None, scratch=()):
    several = isinstance(outs, tuple)
    return pl.pallas_call(
        body,
        out_shape=outs,
        in_specs=in_specs or [VMEM] * len(operands),
        out_specs=out_specs or ((VMEM,) * len(outs) if several else VMEM),
        scratch_shapes=list(scratch),
        compiler_params=pltpu.CompilerParams(vmem_limit_bytes=VMEM_LIMIT),
        cost_estimate=pl.CostEstimate(flops=flops, bytes_accessed=moved, transcendentals=0),
    )(*operands)


def norm_rows(res_ref, gain_ref, hidden_ref, inverse_ref):
    tokens = res_ref.shape[0]
    step = 16

    def norm(i, carry):
        rows = pl.ds(pl.multiple_of(i * step, step), step)
        x = res_ref[rows, :].astype(F32)
        inverse = 1.0 / jnp.sqrt(jnp.mean(x * x, axis=1, keepdims=True) + 1e-06)
        inverse_ref[rows, :] = jnp.broadcast_to(inverse, (step, LANES))
        hidden_ref[rows, :] = (x * inverse * gain_ref[...]).astype(BF16)
        return carry

    lax.fori_loop(0, tokens // step, norm, 0, unroll=16)


def scores_of(table_ref, hidden_ref):
    vocab_rows, block = table_ref.shape[0], 256
    scores = [
        lax.dot_general(
            table_ref[start : min(start + block, vocab_rows), :],
            hidden_ref[...],
            (((1,), (1,)), ((), ())),
            preferred_element_type=F32,
        )
        for start in range(0, vocab_rows, block)
    ]
    scores = jnp.concatenate(scores, axis=0)
    return 30.0 * jnp.tanh(scores * (1.0 / 30.0))


def capped_scores(res_ref, gain_ref, table_ref, hidden_ref, inverse_ref):
    norm_rows(res_ref, gain_ref, hidden_ref, inverse_ref)
    return scores_of(table_ref, hidden_ref)


def logit_grads(capped, first_ref, arrived_ref, targets_ref, mask_ref):
    totals = arrived_ref[0]
    for i in range(1, arrived_ref.shape[0]):
        totals = totals + arrived_ref[i]
    rows = lax.broadcasted_iota(jnp.int32, capped.shape, 0)
    hit = (targets_ref[...] - first_ref[0] == rows).astype(F32)
    share = jnp.exp(capped) * (1.0 / totals)
    bend = capped * (1.0 / 30.0)
    return (mask_ref[...].astype(F32) * (share - hit) * (1.0 - bend * bend)).astype(BF16)


def sums_body(vocab_rows, res_ref, gain_ref, table_ref, sums_ref, hidden_ref, inverse_ref):
    capped = capped_scores(res_ref, gain_ref, table_ref, hidden_ref, inverse_ref)
    rows = lax.broadcasted_iota(jnp.int32, capped.shape, 0)
    sums = jnp.sum(jnp.where(rows < vocab_rows, jnp.exp(capped), 0.0), axis=0, keepdims=True)
    for i in range(sums_ref.shape[0]):
        sums_ref[i] = sums


def spread_body(in_ref, out_ref):
    total = in_ref[0]
    for i in range(1, in_ref.shape[0]):
        total = total + in_ref[i]
    for i in range(out_ref.shape[0]):
        out_ref[i] = total


def partial_body(
    first_ref, arrived_ref, targets_ref, mask_ref, res_ref, gain_ref, table_ref,
    packed_ref, hidden_ref, inverse_ref, rider_ref,
):
    n_plane, own, packed_width = packed_ref.shape
    width = res_ref.shape[1]
    capped = capped_scores(res_ref, gain_ref, table_ref, hidden_ref, inverse_ref)
    dlogits = logit_grads(capped, first_ref, arrived_ref, targets_ref, mask_ref)
    rider_ref[...] = jnp.zeros_like(rider_ref)
    tile = 2 * LANES
    n_lanes = width // LANES
    inverse = jnp.concatenate([inverse_ref[...]] * 2, axis=1)
    for n in range(width // tile):
        columns = slice(n * tile, (n + 1) * tile)
        part = lax.dot_general(
            dlogits, table_ref[:, columns], (((0,), (0,)), ((), ())), preferred_element_type=F32
        )
        packed_ref[:, :, columns] = part.astype(BF16).reshape(n_plane, own, tile)
        normed = res_ref[:, columns].astype(F32) * inverse
        gain = jnp.sum(part * normed, axis=0, keepdims=True)
        high = gain.astype(BF16).astype(F32)
        low = gain - high
        for k in range(2):
            piece = slice(k * LANES, (k + 1) * LANES)
            rider_ref[2 * n + k : 2 * n + k + 1, :] = high[:, piece]
            rider_ref[n_lanes + 2 * n + k : n_lanes + 2 * n + k + 1, :] = low[:, piece]
    for j in range(rider_ref.shape[0] // own):
        block = rider_ref[j * own : (j + 1) * own, :].astype(BF16)
        for i in range(n_plane):
            packed_ref[i, :, width + j * LANES : width + (j + 1) * LANES] = block


def split_body(in_ref, out_ref, gain_ref):
    n_plane, own, packed_width = in_ref.shape
    n_section = out_ref.shape[0]
    cut = out_ref.shape[2] - LANES
    halves = n_section // own
    width = halves * cut
    n_lanes = width // LANES
    total = in_ref[0].astype(F32)
    for i in range(1, n_plane):
        total = total + in_ref[i].astype(F32)
    for h in range(halves):
        out_ref[h * own : (h + 1) * own, 0, :cut] = total[:, h * cut : (h + 1) * cut]
    for j in range((packed_width - width) // LANES):
        gain_ref[j * own : (j + 1) * own, :] = total[:, width + j * LANES : width + (j + 1) * LANES]
    rows = gain_ref[:n_lanes, :] + gain_ref[n_lanes : 2 * n_lanes, :]
    out_ref[:n_lanes, 0, cut:] = rows
    out_ref[n_lanes:, 0, cut:] = jnp.zeros((n_section - n_lanes, LANES), F32)


def finish_body(in_ref, res_ref, gain_ref, grad_ref, grad_gain_ref):
    n_section = in_ref.shape[0]
    own, width = res_ref.shape
    cut = in_ref.shape[2] - LANES
    halves = n_section // own
    x = res_ref[...].astype(F32)
    inverse = 1.0 / jnp.sqrt(jnp.mean(x * x, axis=1, keepdims=True) + 1e-06)
    normed = x * inverse
    grad_hidden = jnp.concatenate(
        [in_ref[h * own : (h + 1) * own, 0, :cut] for h in range(halves)], axis=1
    )
    scaled = grad_hidden * gain_ref[...]
    along = jnp.mean(scaled * normed, axis=1, keepdims=True)
    grad_ref[...] = ((scaled - normed * along) * inverse).astype(BF16)
    grad_gain_ref[...] = in_ref[: width // LANES, 0, cut:]


def table_body(
    first_ref, arrived_ref, targets_ref, mask_ref, res_ref, gain_ref, table_ref, ids_ref,
    cotangent_ref, out_ref, hidden_ref, inverse_ref,
):
    vocab_rows, width = out_ref.shape
    capped = capped_scores(res_ref, gain_ref, table_ref, hidden_ref, inverse_ref)
    dlogits = logit_grads(capped, first_ref, arrived_ref, targets_ref, mask_ref)
    rows = lax.broadcasted_iota(jnp.int32, capped.shape, 0)
    onehot = (ids_ref[...] - first_ref[0] == rows).astype(F32).astype(BF16)
    scale = math.sqrt(width)
    tile = 2 * LANES
    for n in range(width // tile):
        columns = slice(n * tile, (n + 1) * tile)
        head = jnp.dot(dlogits, hidden_ref[:, columns], preferred_element_type=F32)
        inputs = jnp.dot(onehot, cotangent_ref[:, columns], preferred_element_type=F32)
        out_ref[:, columns] = (head + scale * inputs)[:vocab_rows].astype(BF16)


def plan_body(ids_ref, me_ref, rows_ref, codes_ref, pairs_ref, here_ref):
    _, own, groups = ids_ref.shape
    section, place, vocab_rows = me_ref[0], me_ref[1], me_ref[2]
    device = section * groups + place
    lane = lax.broadcasted_iota(jnp.int32, here_ref.shape, 1)
    here_ref[...] = jnp.where(lane == 0, section, jnp.where(lane == 1, place, 0))
    token = lax.broadcasted_iota(jnp.int32, (own, groups), 0)
    group = lax.broadcasted_iota(jnp.int32, (own, groups), 1)

    def column(x):
        return jnp.sum(jnp.where(group == place, x, 0), axis=1, keepdims=True)

    ahead_sent = ahead_here = jnp.zeros((1, groups), jnp.int32)
    for which in range(2):
        ids = ids_ref[which]
        owner = lax.div(ids, vocab_rows)
        again = jnp.zeros(ids.shape, jnp.int32)
        for j in range(own):
            again = again + jnp.where((ids == ids[j : j + 1]) & (token > j), 1, 0)
        first = jnp.where(again == 0, 1, 0)
        slot = jnp.zeros(ids.shape, jnp.int32)
        for j in range(own):
            under = (owner == owner[j : j + 1]) & (ids[j : j + 1] < ids) & (first[j : j + 1] == 1)
            slot = slot + jnp.where(under, 1, 0)
        near = column(owner) - section * groups
        inside = (near >= 0) & (near < groups)
        mine = (owner == device) & (first == 1)
        if which == 0:
            offset = jnp.zeros((own, 1), jnp.int32)
            pair = owner * groups + group
        else:
            offset = jnp.sum(jnp.where(group == near, ahead_sent, 0), axis=1, keepdims=True)
            slot_here = slot + ahead_here
            over = lax.div(owner, groups) * groups
            pair = (over + group) * groups + owner - over
        pairs_ref[which] = jnp.where(first == 1, pair, -1)
        code = jnp.where(inside, (column(slot) + offset) * groups + near, -1)
        codes_ref[which] = jnp.broadcast_to(code, codes_ref.shape[1:])
        rows_ref[which] = jnp.full(rows_ref.shape[1:], -1, jnp.int32)
        for k in range(SLOTS):
            taken = mine & ((slot if which == 0 else slot_here) == k)
            local = jnp.where(taken, ids - device * vocab_rows + 1, 0)
            rows_ref[which, :, k * groups : (k + 1) * groups] = (
                jnp.sum(local, axis=0, keepdims=True) - 1
            )
        if which == 0:
            ahead_sent = jnp.sum(jnp.where(mine, 1, 0), axis=0, keepdims=True)
            come = (group == near) & (column(first) == 1)
            ahead_here = jnp.sum(jnp.where(come, 1, 0), axis=0, keepdims=True)


def three_terms(x):
    high = x.astype(BF16).astype(F32)
    middle = (x - high).astype(BF16).astype(F32)
    return high, middle, x - high - middle


def slot_layout(own, width, tokens):
    n_lanes = width // LANES
    token_tiles = -(-tokens // LANES)
    scalar_tiles = -(-6 * token_tiles // own)
    slot_tiles = -(-SLOTS * n_lanes // own)
    return n_lanes, token_tiles, scalar_tiles, slot_tiles


def slots_body(
    table_ref, slot_rows_ref, codes_ref, cotangent_ref, out_ref, tail_ref, room_ref
):
    n_plane, own, _ = out_ref.shape
    vocab_rows, width = table_ref.shape
    n_lanes, _, _, tiles = slot_layout(own, width, own * n_plane)
    stride = tiles * own

    def put(at, value):
        room_ref[pl.ds(at, n_plane, stride=stride), :] = value

    for at in range(SLOTS * n_lanes, stride):
        put(at, jnp.zeros((n_plane, LANES), F32))
    n_slots = SLOTS * n_plane
    slot_iota = lax.broadcasted_iota(jnp.int32, (vocab_rows, n_slots), 0)
    pick = (slot_rows_ref[0, :, :n_slots] == slot_iota).astype(F32).astype(BF16)
    last = tail_ref.shape[0]
    last_start = (vocab_rows - 1) // last * last
    last_rows = lax.broadcasted_iota(jnp.int32, (vocab_rows, last), 0) - last_start
    pick_last = last_rows == lax.broadcasted_iota(jnp.int32, (vocab_rows, last), 1)
    pick_last = pick_last.astype(F32).astype(BF16)
    own_iota = lax.broadcasted_iota(jnp.int32, (own, n_slots), 1)
    give = (codes_ref[1, :, :n_slots] == own_iota).astype(F32).astype(BF16)
    dims = (((0,), (0,)), ((), ()))
    tile = 2 * LANES
    for n in range(width // tile):
        columns = slice(n * tile, (n + 1) * tile)
        rows = table_ref[:, columns]
        tail_ref[:, columns] = lax.dot_general(
            pick_last, rows, dims, preferred_element_type=F32
        ).astype(BF16)
        moved = lax.dot_general(pick, rows, dims, preferred_element_type=F32)
        moved = moved + lax.dot_general(
            give, cotangent_ref[:, columns], dims, preferred_element_type=F32
        )
        for k in range(SLOTS):
            block = moved[k * n_plane : (k + 1) * n_plane]
            for half in range(2):
                put(k * n_lanes + 2 * n + half, block[:, half * LANES : (half + 1) * LANES])
    for p in range(n_plane):
        for t in range(tiles):
            start = p * stride + t * own
            out_ref[p, :, t * LANES : (t + 1) * LANES] = (
                room_ref[start : start + own, :].astype(BF16)
            )


def whole_rows(table_hbm, table_ref, sem):
    rows = table_ref.shape[0] - 16
    return pltpu.make_async_copy(table_hbm.at[:rows, :], table_ref.at[:rows, :], sem)


def compact_body(
    vocab_rows, here_ref, res_hbm, table_hbm, slots_hbm, tail_ref, gain_ref, targets_ref, mask_ref,
    packed_ref, res_ref, table_ref, slots_ref, hidden_ref, inverse_ref, tokens_ref, room_ref, sems,
):
    copies = [
        pltpu.make_async_copy(res_hbm, res_ref, sems.at[0]),
        whole_rows(table_hbm, table_ref, sems.at[1]),
        pltpu.make_async_copy(slots_hbm, slots_ref, sems.at[2]),
    ]
    for copy in copies:
        copy.start()
    n_plane, own, packed_width = packed_ref.shape
    tokens, width = res_ref.shape
    n_lanes, token_tiles, scalar_tiles, _ = slot_layout(own, width, tokens)
    copies[0].wait()
    norm_rows(res_ref, gain_ref, hidden_ref, inverse_ref)
    copies[1].wait()
    table_ref[table_ref.shape[0] - tail_ref.shape[0] :, :] = tail_ref[...]
    capped = scores_of(table_ref, hidden_ref)
    rows = lax.broadcasted_iota(jnp.int32, capped.shape, 0)
    device = here_ref[:, 0:1] * n_plane + here_ref[:, 1:2]
    hit = targets_ref[...] - device * vocab_rows == rows
    expterm = jnp.where(rows < vocab_rows, jnp.exp(capped), 0.0)
    bend = capped * (1.0 / 30.0)
    weight = mask_ref[...].astype(F32) * (1.0 - bend * bend)
    unscaled = jnp.where(hit, 0.0, weight * expterm).astype(BF16)
    pieces = [
        jnp.sum(expterm, axis=0, keepdims=True),
        jnp.sum(jnp.where(hit, capped, 0.0), axis=0, keepdims=True),
    ]
    tokens_ref[...] = jnp.zeros_like(tokens_ref)
    room_ref[...] = jnp.zeros_like(room_ref)
    for which in range(2):
        for term, value in enumerate(three_terms(pieces[which])):
            tokens_ref[:, :tokens] = value
            for t in range(token_tiles):
                at = (which * 3 + term) * token_tiles + t
                room_ref[at : at + 1, :] = tokens_ref[:, t * LANES : (t + 1) * LANES]
    for t in range(scalar_tiles):
        block = room_ref[t * own : (t + 1) * own, :].astype(BF16)
        for p in range(n_plane):
            packed_ref[p, :, width + t * LANES : width + (t + 1) * LANES] = block
    tile = 2 * LANES
    for n in range(width // tile):
        columns = slice(n * tile, (n + 1) * tile)
        part = lax.dot_general(
            unscaled, table_ref[:, columns], (((0,), (0,)), ((), ())), preferred_element_type=F32
        )
        packed_ref[:, :, columns] = part.astype(BF16).reshape(n_plane, own, tile)
    copies[2].wait()
    packed_ref[:, :, width + scalar_tiles * LANES :] = slots_ref[...]


def unpack_body(
    in_ref, here_ref, codes_ref, out_ref, rows_out_ref, room_ref, moved_ref, rest_ref
):
    n_plane, own, packed_width = in_ref.shape
    tokens = n_plane * own
    n_section = out_ref.shape[0]
    halves = n_section // own
    width = rows_out_ref.shape[1]
    cut = width // halves
    n_lanes, token_tiles, scalar_tiles, slot_tiles = slot_layout(own, width, tokens)
    tiles = scalar_tiles + slot_tiles
    stride = tiles * own
    total = in_ref[0, :, :width].astype(F32)
    for p in range(1, n_plane):
        total = total + in_ref[p, :, :width].astype(F32)
    for p in range(n_plane):
        for t in range(tiles):
            start = p * stride + t * own
            room_ref[start : start + own, :] = in_ref[
                p, :, width + t * LANES : width + (t + 1) * LANES
            ].astype(F32)

    def take(at):
        return room_ref[pl.ds(at, n_plane, stride=stride), :]

    for k in range(SLOTS):
        for j in range(n_lanes):
            moved_ref[k * n_plane : (k + 1) * n_plane, j * LANES : (j + 1) * LANES] = take(
                scalar_tiles * own + k * n_lanes + j
            )
    moved = moved_ref[...].astype(BF16)
    rows_out_ref[...] = moved
    n_slots = SLOTS * n_plane
    own_iota = lax.broadcasted_iota(jnp.int32, (own, n_slots), 1)
    choose = (codes_ref[0, :, :n_slots] == own_iota).astype(F32).astype(BF16)
    target_rows = jnp.dot(choose, moved, preferred_element_type=F32)
    for h in range(halves):
        for i in range(own):
            s = i * halves + h
            rest_ref[2 * s : 2 * s + 1, :cut] = total[i : i + 1, h * cut : (h + 1) * cut]
            rest_ref[2 * s + 1 : 2 * s + 2, :cut] = target_rows[i : i + 1, h * cut : (h + 1) * cut]

    def summed(which):
        tiles_of = []
        for t in range(token_tiles):
            terms = [
                jnp.sum(take((which * 3 + term) * token_tiles + t), axis=0, keepdims=True)
                for term in range(3)
            ]
            tiles_of.append(terms[0] + terms[1] + terms[2])
        return tiles_of

    lane = lax.broadcasted_iota(jnp.int32, (own, LANES), 1)
    token = lax.broadcasted_iota(jnp.int32, (own, LANES), 0) + here_ref[:, 1:2] * own
    score = jnp.zeros((own, 1), F32)
    for t, value in enumerate(summed(1)):
        score = score + jnp.sum(
            jnp.where(lane + t * LANES == token, jnp.broadcast_to(value, lane.shape), 0.0),
            axis=1,
            keepdims=True,
        )
    high, middle, low = three_terms(score)
    scores = jnp.where(lane == 0, high, jnp.where(lane == 1, middle, jnp.where(lane == 2, low, 0.0)))
    sums = [three_terms(value) for value in summed(0)]
    extra = [sums[t][term] for term in range(3) for t in range(token_tiles)]
    per_row = (len(extra) + 2) // 2
    for s in range(n_section):
        i = s // halves
        for n, value in enumerate(extra + [scores[i : i + 1]]):
            row, column = 2 * s + n // per_row, cut + n % per_row * LANES
            rest_ref[row : row + 1, column : column + LANES] = value
        for n in range(len(extra) + 1, 2 * per_row):
            row, column = 2 * s + n // per_row, cut + n % per_row * LANES
            rest_ref[row : row + 1, column : column + LANES] = jnp.zeros((1, LANES), F32)
    for s in range(n_section):
        out_ref[s] = rest_ref[2 * s : 2 * s + 2, :].astype(BF16)


def combine_body(in_ref, here_ref, mask_ref, out_ref, totals_ref, tokens_ref):
    n_section, _, piece_width = in_ref.shape
    cut = out_ref.shape[2]
    tokens = totals_ref.shape[1]
    own = out_ref.shape[0]
    halves = n_section // own
    total = in_ref[0].astype(F32)
    for s in range(1, n_section):
        total = total + in_ref[s].astype(F32)
    token_tiles = -(-tokens // LANES)
    per_row = (piece_width - cut) // LANES

    def tile_of(n):
        row, column = n // per_row, cut + n % per_row * LANES
        return total[row : row + 1, column : column + LANES]

    for t in range(token_tiles):
        tokens_ref[:, t * LANES : (t + 1) * LANES] = (
            tile_of(t) + tile_of(token_tiles + t) + tile_of(2 * token_tiles + t)
        )
    totals = tokens_ref[:, :tokens]
    totals_ref[...] = totals
    token = here_ref[:, 1:2] * own + lax.div(here_ref[:, 0:1], halves)
    here = lax.broadcasted_iota(jnp.int32, totals.shape, 1) == token
    whole = jnp.sum(jnp.where(here, totals, 0.0), axis=1, keepdims=True)
    weight = jnp.sum(jnp.where(here, mask_ref[...].astype(F32), 0.0), axis=1, keepdims=True)
    score = jnp.sum(tile_of(3 * token_tiles), axis=1, keepdims=True)
    bend = score * (1.0 / 30.0)
    at_target = weight * (jnp.exp(score) / whole - 1.0) * (1.0 - bend * bend)
    at_target = at_target.astype(BF16).astype(F32)
    grad = total[0:1, :cut] / whole + at_target * total[1:2, :cut]
    for s in range(out_ref.shape[0]):
        out_ref[s] = grad


def normed_rows(res_ref):
    x = res_ref[...].astype(F32)
    inverse = 1.0 / jnp.sqrt(jnp.mean(x * x, axis=1, keepdims=True) + 1e-06)
    return x * inverse, inverse


def at_left(here_ref, shape):
    return lax.rem(jnp.broadcast_to(here_ref[:, 0:1], shape), 2) == 0


def gain_body(in_ref, here_ref, res_ref, out_ref):
    own, _, cut = in_ref.shape
    normed, _ = normed_rows(res_ref)
    half = jnp.where(at_left(here_ref, (own, cut)), normed[:, :cut], normed[:, cut:])
    gain = jnp.sum(in_ref[:, 0, :] * half, axis=0, keepdims=True)
    for i in range(out_ref.shape[0]):
        out_ref[i] = gain


def close_body(in_ref, other_ref, here_ref, res_ref, gain_ref, grad_ref):
    mine, other = in_ref[:, 0, :], other_ref[:, 0, :]
    first = at_left(here_ref, mine.shape)
    left, right = jnp.where(first, mine, other), jnp.where(first, other, mine)
    normed, inverse = normed_rows(res_ref)
    scaled = jnp.concatenate([left, right], axis=1) * gain_ref[...]
    along = jnp.mean(scaled * normed, axis=1, keepdims=True)
    grad_ref[...] = ((scaled - normed * along) * inverse).astype(BF16)


def compact_table_body(
    here_ref, table_hbm, tail_ref, targets_ref, totals_ref, mask_ref, res_ref, gain_ref, slot_rows_ref,
    moved_ref, out_ref, table_ref, hidden_ref, inverse_ref, sem,
):
    vocab_rows, width = out_ref.shape
    copy = whole_rows(table_hbm, table_ref, sem)
    copy.start()
    norm_rows(res_ref, gain_ref, hidden_ref, inverse_ref)
    copy.wait()
    table_ref[table_ref.shape[0] - tail_ref.shape[0] :, :] = tail_ref[...]
    capped = scores_of(table_ref, hidden_ref)
    rows = lax.broadcasted_iota(jnp.int32, capped.shape, 0)
    device = here_ref[:, 0:1] * (moved_ref.shape[0] // SLOTS) + here_ref[:, 1:2]
    hit = (targets_ref[...] - device * vocab_rows == rows).astype(F32)
    share = jnp.exp(capped) * (1.0 / totals_ref[...])
    bend = capped * (1.0 / 30.0)
    dlogits = (mask_ref[...].astype(F32) * (share - hit) * (1.0 - bend * bend)).astype(BF16)
    n_slots = moved_ref.shape[0]
    slot_iota = lax.broadcasted_iota(jnp.int32, (capped.shape[0], n_slots), 0)
    onehot = (slot_rows_ref[1, :, :n_slots] == slot_iota).astype(F32).astype(BF16)
    scale = math.sqrt(width)
    tile = 2 * LANES
    for n in range(width // tile):
        columns = slice(n * tile, (n + 1) * tile)
        head = jnp.dot(dlogits, hidden_ref[:, columns], preferred_element_type=F32)
        inputs = jnp.dot(onehot, moved_ref[:, columns], preferred_element_type=F32)
        out_ref[:, columns] = (head + scale * inputs)[:vocab_rows].astype(BF16)


def general(
    everyone, plan, residual, final_gain, table, targets, input_ids, loss_mask, embed_cotangent
):
    del plan
    padded = jnp.pad(table, ((0, -table.shape[0] % 16), (0, 0)))
    own, width = residual.shape
    vocab_rows = table.shape[0]
    n_plane, n_section = lax.axis_size(PLANE), lax.axis_size(SECTION)
    tokens = own * n_plane
    cut = own * width // n_section
    n_lanes = width // LANES
    rider = -(-2 * n_lanes // own) * own
    product = 2 * tokens * vocab_rows * width
    shape = jax.ShapeDtypeStruct
    first = (lax.axis_index(EVERY) * vocab_rows).astype(jnp.int32).reshape(1)
    gain_row = final_gain.reshape(1, width)

    packed_width = width + rider // own * LANES
    norm_rooms = [pltpu.VMEM((tokens, width), BF16), pltpu.VMEM((tokens, LANES), F32)]
    rows_bytes = vocab_rows * width * 2

    wide = jnp.pad(embed_cotangent, ((0, 0), (0, 512)))
    all_cotangent = lax.all_gather(wide, PLANE, axis=0, tiled=True)

    sums = call(
        functools.partial(sums_body, vocab_rows),
        shape((n_section, 1, tokens), F32),
        product,
        rows_bytes,
        everyone, gain_row, padded,
        scratch=norm_rooms,
    )
    sums = call(
        spread_body, shape((n_plane, 1, tokens), F32), tokens, 4 * tokens, exchange(sums, SECTION)
    )
    given = (
        first, exchange(sums, PLANE), targets.reshape(1, tokens), loss_mask.reshape(1, tokens),
        everyone, gain_row, padded,
    )
    packed = call(
        partial_body,
        shape((n_plane, own, packed_width), BF16),
        2 * product,
        rows_bytes,
        *given,
        in_specs=[SMEM] + [VMEM] * 6,
        scratch=norm_rooms + [pltpu.VMEM((rider, LANES), F32)],
    )
    arrived = exchange(packed, PLANE)
    split = call(
        split_body,
        shape((n_section, 1, cut + LANES), F32),
        tokens * width,
        tokens * width * 2,
        arrived,
        scratch=[pltpu.VMEM((rider, LANES), F32)],
    )
    reduced = call(
        spread_body,
        shape((n_section, 1, cut + LANES), F32),
        own * width,
        own * width * 8,
        exchange(split, SECTION),
    )
    grad_table = call(
        table_body,
        shape((vocab_rows, width), BF16),
        3 * product,
        2 * rows_bytes,
        *given, input_ids.reshape(1, tokens), all_cotangent,
        in_specs=[SMEM] + [VMEM] * 8,
        scratch=norm_rooms,
    )
    summed, grad_table = lax.optimization_barrier((exchange(reduced, SECTION), grad_table))
    grad_residual, grad_gain = call(
        finish_body,
        (shape((own, width), BF16), shape((n_lanes, LANES), F32)),
        own * width * 10,
        own * width * 8,
        summed, residual, gain_row,
    )
    return (grad_residual, grad_gain.reshape(width), grad_table)


def compact(
    everyone, plan, residual, final_gain, table, targets, input_ids, loss_mask, embed_cotangent
):
    del input_ids, embed_cotangent
    slot_rows, codes, slots, here, tail = plan
    own, width = residual.shape
    vocab_rows = table.shape[0]
    n_plane, n_section = lax.axis_size(PLANE), lax.axis_size(SECTION)
    tokens = own * n_plane
    cut = own * width // n_section
    product = 2 * tokens * vocab_rows * width
    rows_bytes = vocab_rows * width * 2
    shape = jax.ShapeDtypeStruct
    _, token_tiles, scalar_tiles, slot_tiles = slot_layout(own, width, tokens)
    tiles = scalar_tiles + slot_tiles
    packed_width = width + tiles * LANES
    piece_width = cut + (3 * token_tiles + 2) // 2 * LANES
    norm_rooms = [pltpu.VMEM((tokens, width), BF16), pltpu.VMEM((tokens, LANES), F32)]
    gain_row = final_gain.reshape(1, width)
    mask = loss_mask.reshape(1, tokens)
    targets = targets.reshape(1, tokens)

    table_room = pltpu.VMEM((-(-vocab_rows // 16) * 16, width), BF16)
    packed = call(
        functools.partial(compact_body, vocab_rows),
        shape((n_plane, own, packed_width), BF16),
        2 * product,
        rows_bytes,
        here, everyone, table, slots, tail, gain_row, targets, mask,
        in_specs=[VMEM] + [ANY] * 3 + [VMEM] * 4,
        scratch=[
            pltpu.VMEM((tokens, width), BF16),
            table_room,
            pltpu.VMEM((n_plane, own, slot_tiles * LANES), BF16),
        ] + norm_rooms + [
            pltpu.VMEM((1, token_tiles * LANES), F32),
            pltpu.VMEM((scalar_tiles * own, LANES), F32),
            pltpu.SemaphoreType.DMA((3,)),
        ],
    )
    pieces, moved = call(
        unpack_body,
        (
            shape((n_section, 2, piece_width), BF16),
            shape((SLOTS * n_plane, width), BF16),
        ),
        tokens * width,
        tokens * packed_width * 2,
        exchange(packed, PLANE), here, codes,
        scratch=[
            pltpu.VMEM((n_plane * tiles * own, LANES), F32),
            pltpu.VMEM((SLOTS * n_plane, width), F32),
            pltpu.VMEM((2 * n_section, piece_width), F32),
        ],
    )
    half_token, totals = call(
        combine_body,
        (shape((own, 1, cut), F32), shape((1, tokens), F32)),
        own * width,
        own * width * 8,
        exchange(pieces, SECTION), here, mask,
        scratch=[pltpu.VMEM((1, token_tiles * LANES), F32)],
    )
    grad_table = call(
        compact_table_body,
        shape((vocab_rows, width), BF16),
        3 * product,
        2 * rows_bytes,
        here, table, tail, targets, totals, mask, everyone, gain_row, slot_rows, moved,
        in_specs=[VMEM, ANY] + [VMEM] * 8,
        scratch=[table_room] + norm_rooms + [pltpu.SemaphoreType.DMA],
    )
    mine, grad_table = lax.optimization_barrier((exchange(half_token, "z"), grad_table))
    n_chips = lax.axis_size(CHIPS)
    other = lax.ppermute(mine, "core", [(0, 1), (1, 0)])
    gain_part = call(
        gain_body,
        shape((n_chips, 1, cut), F32),
        own * width * 4,
        own * width * 8,
        mine, here, residual,
    )
    grad_residual = call(
        close_body,
        shape((own, width), BF16),
        own * width * 10,
        own * width * 8,
        mine, other, here, residual, gain_row,
    )
    grad_gain = exchange(gain_part, CHIPS).reshape(n_chips // n_plane, n_plane, cut)
    return (grad_residual, jnp.sum(grad_gain, axis=1).reshape(width), grad_table)


def on_device(residual, final_gain, table, targets, input_ids, loss_mask, embed_cotangent):
    own, width = residual.shape
    n_plane = lax.axis_size(PLANE)
    shape = jax.ShapeDtypeStruct
    ids = jnp.stack([targets.reshape(n_plane, own).T, input_ids.reshape(n_plane, own).T])
    place = lax.axis_index(PLANE)
    me = jnp.stack([lax.axis_index(SECTION), place, table.shape[0], own]).astype(jnp.int32)
    lanes = -(-SLOTS * n_plane // LANES) * LANES
    everyone = exchange(jnp.broadcast_to(residual[None], (n_plane, own, width)), PLANE)
    everyone = everyone.reshape(n_plane * own, width)
    slot_rows, codes, pairs, here = call(
        plan_body,
        (
            shape((2, 1, lanes), jnp.int32),
            shape((2, own, lanes), jnp.int32),
            shape((2, own, n_plane), jnp.int32),
            shape((1, LANES), jnp.int32),
        ),
        1000,
        1000,
        ids, me,
        in_specs=[VMEM, SMEM],
    )
    pairs = pairs.reshape(-1)
    alike = (pairs[:, None] == pairs[None, :]) & (pairs[:, None] >= 0)
    fits = jnp.max(jnp.sum(alike.astype(jnp.int32), axis=1)) <= SLOTS
    slot_tiles = slot_layout(own, width, own * n_plane)[3]
    slots, tail = call(
        slots_body,
        (shape((n_plane, own, slot_tiles * LANES), BF16), shape((16, width), BF16)),
        1000,
        1000,
        table, slot_rows, codes, embed_cotangent,
        scratch=[pltpu.VMEM((n_plane * slot_tiles * own, LANES), F32)],
    )
    return lax.cond(
        fits,
        compact,
        general,
        everyone, (slot_rows, codes, slots, here, tail), residual, final_gain, table, targets, input_ids, loss_mask,
        embed_cotangent,
    )


def solution(mesh):
    cores = 2
    devices = mesh.devices.reshape(-1, cores, *mesh.devices.shape[1:])
    fine = jax.sharding.Mesh(devices, EVERY)
    placed = (
        P(PLANE, None),
        P(),
        P(EVERY, None),
        P(),
        P(),
        P(),
        P(PLANE, None),
    )
    return jax.shard_map(
        on_device,
        mesh=fine,
        in_specs=placed,
        out_specs=(P(PLANE, None), P(), P(EVERY, None)),
        check_vma=False,
    )
```
